512 devices in a mesh: inst: 64 (over z, y), tp: 8 (over x, core).
Axes of the slice: x: 4, y: 4, z: 16, core: 2. Of those that a mesh axis runs over, the one named last changes fastest.
Arguments:
- anchor: int32 [1024], P('inst'), may hold values from 0 to 1023, as said below
- target: int32 [1024], P('inst'), may hold values from 0 to 1023, as said below
- ssm_state: float32 [1024, 16, 8192], P('inst', None, 'tp'), may hold values from -0.04 to 0.04
- conv_state: float32 [1024, 3, 8192], P('inst', None, 'tp'), may hold values from -6 to 6
- x_in: bfloat16 [1024, 2, 8192], P('inst', None, 'tp'), may hold values from -6 to 6
- gate_in: bfloat16 [1024, 2, 8192], P('inst', None, 'tp'), may hold values from -6 to 6
- conv_weight: float32 [4, 8192], P(None, 'tp'), may hold values from -3 to 3
- x_weight: bfloat16 [8192, 544], P('tp'), may hold values from -0.0625 to 0.0625
- dt_weight: bfloat16 [512, 8192], P(None, 'tp'), may hold values from -0.25 to 0.25
- dt_bias: float32 [8192], P('tp'), may hold values from -5 to -3
- a_log: float32 [16, 8192], P(None, 'tp'), may hold values from 0 to 2.5
- d_skip: float32 [8192], P('tp'), may hold values from 0.5 to 1.5
- dt_gain: float32 [512], replicated, may hold values from 0.25 to 1.75
Outputs:
- mixed: bfloat16 [1024, 2, 8192], P('inst', None, 'tp')
- ssm_final: float32 [1024, 16, 8192], P('inst', None, 'tp')
The draws below stay inside these ranges and needn't reach their ends.
Inputs may be any that keep to these rules, and one draw needn't show every extreme that they name: `anchor`: a permutation of the slots; the slots of one instance take states of at most one slot of any other instance, and exactly 12 of them take states from other instances; the offsets, modulo 64, from the sending instance to the receiving one are the same 12 distinct nonzero offsets for every instance. `target`: the inverse permutation of anchor.
All inputs are finite; a program needn't handle non-finite values.
Results may differ from the reference program's by a relative error of at most 0.013.
Values sent between devices are 32-bit elements; how exact they have to be, the bound alone decides.
No kernel may reach another device: no remote copies, remote signals or barrier semaphores. Data moves between devices by JAX's collectives and lax.ppermute only.
A program may use at most 64 MiB of HBM per device.

```python
import jax
import jax.numpy as jnp
from jax import lax

INNER = 8192
NS = 16
DTR = 512
KW = 4
STEPS = 2
SLOTS = 16
GROUPS = 12
ALL_SLOTS = 1024


def migration(key):
    first, second = jax.random.split(key)
    instances = ALL_SLOTS // SLOTS
    shifts = 1 + jax.random.permutation(first, instances - 1)[:GROUPS]
    orders = jax.vmap(lambda item: jax.random.permutation(item, SLOTS))(jax.random.split(second, instances))
    sources = (jnp.arange(instances)[:, None] - shifts[None, :]) % instances
    columns = jnp.broadcast_to(jnp.arange(GROUPS)[None, :], (instances, GROUPS))
    dst_index = jnp.arange(instances)[:, None] * SLOTS + orders[:, :GROUPS]
    src_index = sources * SLOTS + orders[sources, columns]
    anchor = jnp.arange(ALL_SLOTS, dtype=jnp.int32).at[dst_index.reshape(-1)].set(src_index.reshape(-1).astype(jnp.int32))
    target = jnp.zeros((ALL_SLOTS,), jnp.int32).at[anchor].set(jnp.arange(ALL_SLOTS, dtype=jnp.int32))
    return (anchor.astype(jnp.int32), target.astype(jnp.int32))


def draw_anchor(key, part):
    return migration(key)[0]


def draw_target(key, part):
    return migration(key)[1]


def block_scale(stream_key, dims, cuts, low, largest):
    factor_of = 1.0
    for dim, shards_of in cuts:
        heights = jax.random.uniform(jax.random.fold_in(jax.random.fold_in(stream_key, 6), dim), (shards_of,), jnp.float32, low / len(cuts), largest / len(cuts))
        factor_of = factor_of * jnp.repeat(jnp.exp(heights), dims[dim] // shards_of).reshape((-1,) + (1,) * (len(dims) - 1 - dim))
    return factor_of


def centred(own_key, extent, width, limit, shards=(), held_as=jnp.bfloat16):
    drawn = jax.random.normal(own_key, extent, jnp.float32) * width
    if len(shards) > 0:
        drawn = block_scale(own_key, extent, shards, -0.22, 0.18) * drawn
    return jnp.clip(drawn, min=-limit, max=limit).astype(held_as)


def setup_inputs(seed: int = 0) -> dict:
    arg_keys = jax.random.split(jax.random.key(seed), 14)
    return {
        "anchor": draw_anchor(jax.random.fold_in(arg_keys[13], 71), 0),
        "target": draw_target(jax.random.fold_in(arg_keys[13], 71), 0),
        "ssm_state": jnp.clip(jax.random.uniform(arg_keys[2], (ALL_SLOTS, NS, INNER), jnp.float32, -0.04, 0.04) * block_scale(arg_keys[2], (ALL_SLOTS, NS, INNER), ((0, 64), (2, 8)), -0.4, 0.0), -0.04, 0.04),
        "conv_state": centred(arg_keys[3], (ALL_SLOTS, KW - 1, INNER), 1.0, 6.0, ((0, 64), (2, 8)), jnp.float32),
        "x_in": centred(arg_keys[4], (ALL_SLOTS, STEPS, INNER), 1.0, 6.0, ((0, 64), (2, 8))),
        "gate_in": centred(arg_keys[5], (ALL_SLOTS, STEPS, INNER), 1.0, 6.0, ((0, 64), (2, 8))),
        "conv_weight": centred(arg_keys[6], (KW, INNER), KW ** -0.5, 3.0, ((1, 8),), jnp.float32),
        "x_weight": centred(arg_keys[7], (INNER, DTR + 2 * NS), INNER ** -0.5, 0.0625, ((0, 8),)),
        "dt_weight": centred(arg_keys[8], (DTR, INNER), DTR ** -0.5, 0.25, ((1, 8),)),
        "dt_bias": jnp.clip(-5.0 + 2.0 * jax.random.uniform(arg_keys[9], (INNER,), jnp.float32) ** block_scale(arg_keys[9], (INNER,), ((0, 8),), -0.2, 0.2), -5.0, -3.0),
        "a_log": jnp.clip(2.5 * jax.random.uniform(arg_keys[10], (NS, INNER), jnp.float32) ** block_scale(arg_keys[10], (NS, INNER), ((1, 8),), -0.2, 0.2), 0.0, 2.5),
        "d_skip": jnp.clip(0.5 + 1.0 * jax.random.uniform(arg_keys[11], (INNER,), jnp.float32) ** block_scale(arg_keys[11], (INNER,), ((0, 8),), -0.2, 0.2), 0.5, 1.5),
        "dt_gain": jnp.clip(1.0 + 0.15 * jax.random.normal(arg_keys[12], (DTR,), jnp.float32), 0.25, 1.75),
    }


def decode(state, conv_rows, x_in, gate_in, conv_weight, x_weight, dt_weight, dt_bias, a_log, d_skip, dt_gain):
    decay_rates = jnp.exp(a_log)
    results = []
    for step_index in range(STEPS):
        window = jnp.concatenate([conv_rows, x_in[:, step_index:step_index + 1].astype(jnp.float32)], axis=1)
        conved = jax.nn.silu(lax.optimization_barrier(jnp.sum(window * conv_weight[None], axis=1))).astype(jnp.bfloat16)
        conv_rows = window[:, 1:]
        projected = jnp.dot(conved, x_weight, preferred_element_type=jnp.float32)
        dt_part = projected[:, :DTR]
        inv_rms = lax.rsqrt(lax.optimization_barrier(jnp.mean(dt_part * dt_part, axis=-1, keepdims=True)) + 1e-06)
        dt_low = (dt_part * inv_rms * dt_gain).astype(jnp.bfloat16)
        b_vector = projected[:, DTR:DTR + NS]
        c_vector = projected[:, DTR + NS:]
        step_size = jax.nn.softplus(jnp.dot(dt_low, dt_weight, preferred_element_type=jnp.float32) + dt_bias)
        x_values = conved.astype(jnp.float32)
        state = jnp.exp(-step_size[:, None, :] * decay_rates[None]) * state + (step_size * x_values)[:, None, :] * b_vector[:, :, None]
        y_output = lax.optimization_barrier(jnp.sum(c_vector[:, :, None] * state, axis=1)) + d_skip * x_values
        gate_values = jax.nn.silu(gate_in[:, step_index].astype(jnp.float32))
        results.append((y_output * gate_values).astype(jnp.bfloat16))
    return (jnp.stack(results, axis=1), state)

def reference(anchor, target, ssm_state, conv_state, x_in, gate_in, conv_weight, x_weight, dt_weight, dt_bias, a_log, d_skip, dt_gain):
    state = jnp.zeros_like(ssm_state).at[target].set(ssm_state)
    conv_rows = conv_state[anchor]
    mixed, ssm_final = decode(state, conv_rows, x_in, gate_in, conv_weight, x_weight, dt_weight, dt_bias, a_log, d_skip, dt_gain)
    return (mixed, ssm_final)
```

```python
import functools

import jax
import jax.numpy as jnp
import numpy as np
from jax import lax
from jax.experimental import pallas as pl
from jax.experimental.pallas import tpu as pltpu
from jax.sharding import PartitionSpec as P

DTR = 512
GROUPS = 12
VMEM = pl.BlockSpec(memory_space=pltpu.VMEM)
SMEM = pl.BlockSpec(memory_space=pltpu.SMEM)

FIRST = 6
CONV = GROUPS // 4
YS = 4


def pack_kernel(me_ref, anchor_ref, target_ref, state_ref, conv_ref, taps_ref, a_ref, b_ref, offset_ref, row_ref, slot_of, rank_of, source):
    slots = state_ref.shape[0]
    peers = slot_of.shape[0]
    me = me_ref[0]
    for o in range(peers):
        slot_of[o] = -1
    for s in range(slots):
        slot_of[(target_ref[s] // slots - me + peers) % peers] = s
    rank = jnp.int32(0)
    for k in range(16):
        offset_ref[k] = 0
    for o in range(1, peers):
        slot = slot_of[o]
        rank_of[o] = rank
        offset_ref[rank] = o
        source[rank] = slot
        rank = rank + (slot >= 0).astype(jnp.int32)
    for s in range(slots):
        offset = (me - anchor_ref[s] // slots + peers) % peers
        row_ref[s] = jnp.where(offset == 0, GROUPS + anchor_ref[s] % slots, rank_of[offset])

    taps = [taps_ref[i : i + 1, :] for i in range(3)]
    for k in range(GROUPS):
        slot = source[k]
        for t in range(16):
            rows, lanes = 8 * (t // 8), 128 * (t % 8)
            block = state_ref[slot, rows : rows + 8, lanes : lanes + 128]
            for h in range(2):
                if k < FIRST:
                    a_ref[t, CONV + 2 * k + h] = block[4 * h : 4 * h + 4]
                else:
                    b_ref[t, 2 * (k - FIRST) + h] = block[4 * h : 4 * h + 4]
        old = [conv_ref[slot, i : i + 1, :] for i in range(3)]
        sums = (old[0] * taps[0] + old[1] * taps[1] + old[2] * taps[2], old[1] * taps[0] + old[2] * taps[1])
        for t in range(16):
            lanes = 128 * (t % 8)
            a_ref[t, k // 4, k % 4 : k % 4 + 1, :] = sums[t // 8][:, lanes : lanes + 128]


def pack(me, anchor, target, ssm_state, conv_state, conv_weight, peers):
    zs = peers // YS
    return pl.pallas_call(
        pack_kernel,
        out_shape=(
            jax.ShapeDtypeStruct((zs, CONV + 2 * FIRST, 4, 128), jnp.float32),
            jax.ShapeDtypeStruct((zs, 2 * (GROUPS - FIRST), 4, 128), jnp.float32),
            jax.ShapeDtypeStruct((16,), jnp.int32),
            jax.ShapeDtypeStruct((16,), jnp.int32),
        ),
        in_specs=[SMEM, SMEM, SMEM, VMEM, VMEM, VMEM],
        out_specs=(VMEM, VMEM, SMEM, SMEM),
        scratch_shapes=[pltpu.SMEM((peers,), jnp.int32), pltpu.SMEM((peers,), jnp.int32), pltpu.SMEM((16,), jnp.int32)],
        compiler_params=pltpu.CompilerParams(vmem_limit_bytes=32 << 20),
        name="pack",
    )(me, anchor, target, ssm_state, conv_state, conv_weight)


def turn_kernel(conv_groups, first, me_ref, offset_ref, held_ref, came_ref, out_ref):
    zs = held_ref.shape[0]
    y = me_ref[0] % YS
    line = lax.broadcasted_iota(jnp.int32, (4, 128), 0)

    def plan(k):
        offset = offset_ref[k]
        return offset // 2 % 2 == 1, (offset + (y - offset + peers) % YS) // YS

    peers = zs * YS

    def pick(rank_plan, z, group):
        came, hops = rank_plan
        sender = (z - hops + zs) % zs
        return jnp.where(came, came_ref[sender, group], held_ref[sender, group])

    for q in range(conv_groups):
        plans = [plan(4 * q + m) for m in range(4)]
        for z in range(zs):
            rows = [pick(p, z, q) for p in plans]
            out_ref[z, q] = jnp.where(
                line < 2, jnp.where(line == 0, rows[0], rows[1]), jnp.where(line == 2, rows[2], rows[3])
            )
    for k in range((held_ref.shape[1] - conv_groups) // 2):
        rank_plan = plan(first + k)
        for z in range(zs):
            for h in range(2):
                group = conv_groups + 2 * k + h
                out_ref[z, group] = pick(rank_plan, z, group)


def turn(conv_groups, first, me, offset, held, came):
    return pl.pallas_call(
        functools.partial(turn_kernel, conv_groups, first),
        out_shape=jax.ShapeDtypeStruct(held.shape, jnp.float32),
        in_specs=[SMEM, SMEM, VMEM, VMEM],
        out_specs=VMEM,
        compiler_params=pltpu.CompilerParams(vmem_limit_bytes=32 << 20),
        name="turn",
    )(me, offset, held, came)


def along_y(conv_groups, first, me, offset, held):
    peers = lax.axis_size("inst")

    def shift(array, by):
        return lax.ppermute(array, "inst", [(i, i // YS * YS + (i + by) % YS) for i in range(peers)])

    ranks = [[4 * q + m for m in range(4)] for q in range(conv_groups)]
    ranks += [[first + g // 2] * 4 for g in range(held.shape[1] - conv_groups)]
    odd = (offset % 2 == 1)[np.array(ranks)]
    held = jnp.where(odd[None, :, :, None], shift(held, 1), held)
    return turn(conv_groups, first, me, offset, held, shift(held, 2))


def along_z(chunks):
    peers = lax.axis_size("inst")
    groups = [list(range(y, peers, YS)) for y in range(YS)]
    return lax.all_to_all(chunks, "inst", 0, 0, axis_index_groups=groups)


def update_kernel(row_ref, first_ref, second_ref, state_ref, step_ref, x_ref, b_ref, c_ref, decay_ref, skip_ref, gate_ref, mixed_ref, out_ref, held, y_ref):
    slots, state_size, width = state_ref.shape
    steps = step_ref.shape[0]
    for s in range(slots):
        r = row_ref[s]

        def gather(get):
            for t in range(16):
                rows, lanes = 8 * (t // 8), 128 * (t % 8)
                held[s, rows : rows + 8, lanes : lanes + 128] = get(t)

        @pl.when(r < FIRST)
        def _():
            group = CONV + 2 * jnp.minimum(r, FIRST - 1)
            gather(lambda t: jnp.concatenate([first_ref[t, group], first_ref[t, group + 1]]))

        @pl.when((r >= FIRST) & (r < GROUPS))
        def _():
            group = 2 * jnp.clip(r - FIRST, 0, GROUPS - FIRST - 1)
            gather(lambda t: jnp.concatenate([second_ref[t, group], second_ref[t, group + 1]]))

        @pl.when(r >= GROUPS)
        def _():
            held[s] = state_ref[jnp.maximum(r - GROUPS, 0)]

    for s in range(slots):
        b = [b_ref[i, :, s : s + 1] for i in range(steps)]
        c = [c_ref[i, :, s : s + 1] for i in range(steps)]
        for lanes in range(0, width, 128):
            cut = slice(lanes, lanes + 128)
            state = held[s, :, cut]
            decay = decay_ref[:, cut]
            for i in range(steps):
                step = step_ref[i, s : s + 1, cut]
                state = jnp.exp(-step * decay) * state + (step * x_ref[i, s : s + 1, cut]) * b[i]
                y_ref[i, s : s + 1, cut] = jnp.sum(c[i] * state, axis=0, keepdims=True)
            out_ref[s, :, cut] = state
    for i in range(steps):
        gate = gate_ref[i]
        mixed_ref[i] = ((y_ref[i] + skip_ref[...] * x_ref[i]) * jax.nn.silu(gate)).astype(mixed_ref.dtype)


def update(row, first, second, state, step, x, b, c, decay, skip, gate):
    steps, slots, width = step.shape
    return pl.pallas_call(
        update_kernel,
        out_shape=(
            jax.ShapeDtypeStruct(step.shape, jnp.bfloat16),
            jax.ShapeDtypeStruct(state.shape, jnp.float32),
        ),
        in_specs=[SMEM] + [VMEM] * 10,
        out_specs=(VMEM, VMEM),
        scratch_shapes=[pltpu.VMEM(state.shape, jnp.float32), pltpu.VMEM(step.shape, jnp.float32)],
        compiler_params=pltpu.CompilerParams(vmem_limit_bytes=32 << 20),
        name="update",
    )(row, first, second, state, step, x, b, c, decay, skip, gate)


def sum_over_tp(part):
    half = part.shape[0] // 2
    size = lax.axis_size("tp")
    first = lax.axis_index("tp") % 2 == 0

    def swap(array, bit):
        return lax.ppermute(array, "tp", [(i, i ^ bit) for i in range(size)])

    mine = jnp.where(first, part[:half], part[half:]) + swap(jnp.where(first, part[half:], part[:half]), 1)
    bit = 2
    while bit < size:
        mine = mine + swap(mine, bit)
        bit *= 2
    other = swap(mine, 1)
    return jnp.concatenate([jnp.where(first, mine, other), jnp.where(first, other, mine)])


def local(
    anchor,
    target,
    ssm_state,
    conv_state,
    x_in,
    gate_in,
    conv_weight,
    x_weight,
    dt_weight,
    dt_bias,
    a_log,
    d_skip,
    dt_gain,
):
    slots, state_size, width = ssm_state.shape
    steps = x_in.shape[1]
    taps = conv_weight.shape[0]
    peers = lax.axis_size("inst")
    me = lax.axis_index("inst").astype(jnp.int32).reshape(1)

    first, second, offset, row = pack(me, anchor, target, ssm_state, conv_state, conv_weight, peers)
    first = along_z(first)
    second, first = lax.optimization_barrier((second, first))
    second = along_z(second)
    second, first = lax.optimization_barrier((second, along_y(CONV, 0, me, offset, first)))
    first = along_z(first)
    second, first = lax.optimization_barrier((along_y(0, FIRST, me, offset, second), first))
    second = along_z(second)

    stayed = jnp.stack(
        [
            jnp.sum(conv_state[:, i:] * conv_weight[None, : taps - 1 - i], axis=1)
            for i in range(steps)
        ],
        axis=1,
    )
    came = first[:, :CONV].reshape(steps, -1, GROUPS, 128).transpose(2, 0, 1, 3).reshape(GROUPS, steps, width)
    partial = jnp.take(jnp.concatenate([came, stayed]), row, axis=0)
    x_values = x_in.astype(jnp.float32)
    conved = []
    for i in range(steps):
        window = partial[:, i] + jnp.sum(x_values[:, : i + 1] * conv_weight[None, taps - 1 - i :], axis=1)
        conved.append(jax.nn.silu(window).astype(jnp.bfloat16))
    conved = jnp.concatenate(conved, axis=0)
    totals = sum_over_tp(jnp.dot(conved, x_weight, preferred_element_type=jnp.float32))
    dt_part = totals[:, :DTR]
    inv_rms = lax.rsqrt(jnp.mean(dt_part * dt_part, axis=-1, keepdims=True) + 1e-06)
    dt_low = (dt_part * inv_rms * dt_gain).astype(jnp.bfloat16)
    step_size = jax.nn.softplus(jnp.dot(dt_low, dt_weight, preferred_element_type=jnp.float32) + dt_bias)
    rest = totals[:, DTR:].reshape(steps, slots, 2 * state_size).transpose(0, 2, 1)
    mixed, state = update(
        row,
        first,
        second,
        ssm_state,
        step_size.reshape(steps, slots, width),
        conved.astype(jnp.float32).reshape(steps, slots, width),
        rest[:, :state_size],
        rest[:, state_size:],
        jnp.exp(a_log),
        d_skip.reshape(1, width),
        gate_in.astype(jnp.float32).transpose(1, 0, 2),
    )
    return mixed.transpose(1, 0, 2), state


def solution(mesh):
    return jax.shard_map(
        local,
        mesh=mesh,
        in_specs=(
            P("inst"),
            P("inst"),
            P("inst", None, "tp"),
            P("inst", None, "tp"),
            P("inst", None, "tp"),
            P("inst", None, "tp"),
            P(None, "tp"),
            P("tp", None),
            P(None, "tp"),
            P("tp"),
            P(None, "tp"),
            P("tp"),
            P(),
        ),
        out_specs=(P("inst", None, "tp"), P("inst", None, "tp")),
        check_vma=False,
    )
```

```python
import functools

import jax
import jax.numpy as jnp
import numpy as np
from jax import lax
from jax.experimental import pallas as pl
from jax.experimental.pallas import tpu as pltpu
from jax.sharding import PartitionSpec as P

DTR = 512
GROUPS = 12
VMEM = pl.BlockSpec(memory_space=pltpu.VMEM)
SMEM = pl.BlockSpec(memory_space=pltpu.SMEM)

def peer_order(peers):
    zs = peers // 4
    bits = zs.bit_length() - 1
    order = []
    for place in range(peers):
        low = place % zs
        z = sum((low >> i & 1) << (bits - 1 - i) for i in range(bits))
        order.append(4 * z + (place // zs + place) % 4)
    return order


def pack_kernel(me_ref, anchor_ref, target_ref, state_ref, conv_ref, taps_ref, leaving_ref, offset_ref, row_ref, slot_of, rank_of, source):
    slots, state_size, width = state_ref.shape
    peers = leaving_ref.shape[0]
    me = me_ref[0]
    for o in range(peers):
        slot_of[o] = -1
    for s in range(slots):
        slot_of[(target_ref[s] // slots - me + peers) % peers] = s
    rank = jnp.int32(0)
    for k in range(16):
        offset_ref[k] = 0
    for o in range(1, peers):
        slot = slot_of[o]
        rank_of[o] = rank
        offset_ref[rank] = o
        source[rank] = slot
        rank = rank + (slot >= 0).astype(jnp.int32)
    for s in range(slots):
        offset = (me - anchor_ref[s] // slots + peers) % peers
        row_ref[s] = jnp.where(offset == 0, GROUPS + anchor_ref[s] % slots, rank_of[offset])

    taps = [taps_ref[i : i + 1, :] for i in range(3)]
    for k in range(GROUPS):
        slot = source[k]
        for t in range(16):
            tile = 16 * k + t
            rows, lanes = 8 * (t // 8), 128 * (t % 8)
            block = state_ref[slot, rows : rows + 8, lanes : lanes + 128]
            for h in range(2):
                leaving_ref[tile % peers, 2 * (tile // peers) + h] = block[4 * h : 4 * h + 4]
        old = [conv_ref[slot, i : i + 1, :] for i in range(3)]
        sums = (old[0] * taps[0] + old[1] * taps[1] + old[2] * taps[2], old[1] * taps[0] + old[2] * taps[1])
        for i in range(2):
            for c in range(8):
                r = 16 * k + 8 * i + c
                leaving_ref[r // 3, 6, r % 3 : r % 3 + 1, :] = sums[i][:, 128 * c : 128 * c + 128]


def pack(me, anchor, target, ssm_state, conv_state, conv_weight, peers):
    return pl.pallas_call(
        pack_kernel,
        out_shape=(
            jax.ShapeDtypeStruct((peers, 7, 4, 128), jnp.float32),
            jax.ShapeDtypeStruct((16,), jnp.int32),
            jax.ShapeDtypeStruct((16,), jnp.int32),
        ),
        in_specs=[SMEM, SMEM, SMEM, VMEM, VMEM, VMEM],
        out_specs=(VMEM, SMEM, SMEM),
        scratch_shapes=[pltpu.SMEM((peers,), jnp.int32), pltpu.SMEM((peers,), jnp.int32), pltpu.SMEM((16,), jnp.int32)],
        compiler_params=pltpu.CompilerParams(vmem_limit_bytes=32 << 20),
        name="pack",
    )(me, anchor, target, ssm_state, conv_state, conv_weight)


def roll_kernel(order, me_ref, place_ref, offset_ref, held_ref, first_ref, second_ref):
    peers = held_ref.shape[0]
    place = place_ref[me_ref[0]]
    state_shift = [offset_ref[4 * u + place // 16] for u in range(3)]
    conv_shift = [offset_ref[(3 * place + m) // 16] for m in range(3)]
    line = lax.broadcasted_iota(jnp.int32, (4, 128), 0)
    for d in range(peers):
        sender = [place_ref[(order[d] - shift + peers) % peers] for shift in state_shift]
        rows = [held_ref[place_ref[(order[d] - shift + peers) % peers], 6] for shift in conv_shift]
        first_ref[d, 0] = jnp.where(line == 0, rows[0], jnp.where(line == 1, rows[1], rows[2]))
        for h in range(2):
            first_ref[d, 1 + h] = held_ref[sender[0], h]
            second_ref[d, h] = held_ref[sender[1], 2 + h]
            second_ref[d, 2 + h] = held_ref[sender[2], 4 + h]


def roll(me, offset, held):
    peers = held.shape[0]
    order = peer_order(peers)
    return pl.pallas_call(
        functools.partial(roll_kernel, order),
        out_shape=(
            jax.ShapeDtypeStruct((peers, 3, 4, 128), jnp.float32),
            jax.ShapeDtypeStruct((peers, 4, 4, 128), jnp.float32),
        ),
        in_specs=[SMEM, SMEM, SMEM, VMEM],
        out_specs=(VMEM, VMEM),
        compiler_params=pltpu.CompilerParams(vmem_limit_bytes=32 << 20),
        name="roll",
    )(me, jnp.array(np.argsort(order), jnp.int32), offset, held)


def update_kernel(row_ref, first_ref, second_ref, state_ref, step_ref, x_ref, b_ref, c_ref, decay_ref, skip_ref, gate_ref, mixed_ref, out_ref, held, y_ref):
    slots, state_size, width = state_ref.shape
    steps = step_ref.shape[0]
    for s in range(slots):
        r = row_ref[s]

        def gather(get):
            for t in range(16):
                rows, lanes = 8 * (t // 8), 128 * (t % 8)
                held[s, rows : rows + 8, lanes : lanes + 128] = get(t)

        @pl.when(r < 4)
        def _():
            base = jnp.minimum(r, 3) * 16
            gather(lambda t: jnp.concatenate([first_ref[base + t, 1], first_ref[base + t, 2]]))

        @pl.when((r >= 4) & (r < GROUPS))
        def _():
            place = jnp.clip(r - 4, 0, 7)
            base = place % 4 * 16
            half = place // 4 * 2
            gather(lambda t: jnp.concatenate([second_ref[base + t, half], second_ref[base + t, half + 1]]))

        @pl.when(r >= GROUPS)
        def _():
            held[s] = state_ref[jnp.maximum(r - GROUPS, 0)]

    for s in range(slots):
        b = [b_ref[i, :, s : s + 1] for i in range(steps)]
        c = [c_ref[i, :, s : s + 1] for i in range(steps)]
        for lanes in range(0, width, 128):
            cut = slice(lanes, lanes + 128)
            state = held[s, :, cut]
            decay = decay_ref[:, cut]
            for i in range(steps):
                step = step_ref[i, s : s + 1, cut]
                state = jnp.exp(-step * decay) * state + (step * x_ref[i, s : s + 1, cut]) * b[i]
                y_ref[i, s : s + 1, cut] = jnp.sum(c[i] * state, axis=0, keepdims=True)
            out_ref[s, :, cut] = state
    for i in range(steps):
        gate = gate_ref[i]
        mixed_ref[i] = ((y_ref[i] + skip_ref[...] * x_ref[i]) * jax.nn.silu(gate)).astype(mixed_ref.dtype)


def update(row, first, second, state, step, x, b, c, decay, skip, gate):
    steps, slots, width = step.shape
    return pl.pallas_call(
        update_kernel,
        out_shape=(
            jax.ShapeDtypeStruct(step.shape, jnp.bfloat16),
            jax.ShapeDtypeStruct(state.shape, jnp.float32),
        ),
        in_specs=[SMEM] + [VMEM] * 10,
        out_specs=(VMEM, VMEM),
        scratch_shapes=[pltpu.VMEM(state.shape, jnp.float32), pltpu.VMEM(step.shape, jnp.float32)],
        compiler_params=pltpu.CompilerParams(vmem_limit_bytes=32 << 20),
        name="update",
    )(row, first, second, state, step, x, b, c, decay, skip, gate)


def exchange(chunks):
    return lax.all_to_all(chunks, "inst", 0, 0, axis_index_groups=[peer_order(chunks.shape[0])])


def sum_over_tp(part):
    half = part.shape[0] // 2
    size = lax.axis_size("tp")
    first = lax.axis_index("tp") % 2 == 0

    def swap(array, bit):
        return lax.ppermute(array, "tp", [(i, i ^ bit) for i in range(size)])

    mine = jnp.where(first, part[:half], part[half:]) + swap(jnp.where(first, part[half:], part[:half]), 1)
    bit = 2
    while bit < size:
        mine = mine + swap(mine, bit)
        bit *= 2
    other = swap(mine, 1)
    return jnp.concatenate([jnp.where(first, mine, other), jnp.where(first, other, mine)])


def local(
    anchor,
    target,
    ssm_state,
    conv_state,
    x_in,
    gate_in,
    conv_weight,
    x_weight,
    dt_weight,
    dt_bias,
    a_log,
    d_skip,
    dt_gain,
):
    slots, state_size, width = ssm_state.shape
    steps = x_in.shape[1]
    taps = conv_weight.shape[0]
    peers = lax.axis_size("inst")
    me = lax.axis_index("inst").astype(jnp.int32).reshape(1)

    leaving, offset, row = pack(me, anchor, target, ssm_state, conv_state, conv_weight, peers)
    first, second = roll(me, offset, exchange(leaving))
    first = exchange(first)
    second, first = lax.optimization_barrier((second, first))
    second = exchange(second)

    stayed = jnp.stack(
        [
            jnp.sum(conv_state[:, i:] * conv_weight[None, : taps - 1 - i], axis=1)
            for i in range(steps)
        ],
        axis=1,
    )
    came = first[:, 0, :3].reshape(GROUPS, steps, width)
    partial = jnp.take(jnp.concatenate([came, stayed]), row, axis=0)
    x_values = x_in.astype(jnp.float32)
    conved = []
    for i in range(steps):
        window = partial[:, i] + jnp.sum(x_values[:, : i + 1] * conv_weight[None, taps - 1 - i :], axis=1)
        conved.append(jax.nn.silu(window).astype(jnp.bfloat16))
    conved = jnp.concatenate(conved, axis=0)
    totals = sum_over_tp(jnp.dot(conved, x_weight, preferred_element_type=jnp.float32))
    dt_part = totals[:, :DTR]
    inv_rms = lax.rsqrt(jnp.mean(dt_part * dt_part, axis=-1, keepdims=True) + 1e-06)
    dt_low = (dt_part * inv_rms * dt_gain).astype(jnp.bfloat16)
    step_size = jax.nn.softplus(jnp.dot(dt_low, dt_weight, preferred_element_type=jnp.float32) + dt_bias)
    rest = totals[:, DTR:].reshape(steps, slots, 2 * state_size).transpose(0, 2, 1)
    mixed, state = update(
        row,
        first,
        second,
        ssm_state,
        step_size.reshape(steps, slots, width),
        conved.astype(jnp.float32).reshape(steps, slots, width),
        rest[:, :state_size],
        rest[:, state_size:],
        jnp.exp(a_log),
        d_skip.reshape(1, width),
        gate_in.astype(jnp.float32).transpose(1, 0, 2),
    )
    return mixed.transpose(1, 0, 2), state


def solution(mesh):
    return jax.shard_map(
        local,
        mesh=mesh,
        in_specs=(
            P("inst"),
            P("inst"),
            P("inst", None, "tp"),
            P("inst", None, "tp"),
            P("inst", None, "tp"),
            P("inst", None, "tp"),
            P(None, "tp"),
            P("tp", None),
            P(None, "tp"),
            P("tp"),
            P(None, "tp"),
            P("tp"),
            P(),
        ),
        out_specs=(P("inst", None, "tp"), P("inst", None, "tp")),
        check_vma=False,
    )
```

```python
import jax
import jax.numpy as jnp
from jax import lax
from jax.experimental import pallas as pl
from jax.experimental.pallas import tpu as pltpu
from jax.sharding import PartitionSpec as P

DTR = 512
GROUPS = 12
VMEM = pl.BlockSpec(memory_space=pltpu.VMEM)
SMEM = pl.BlockSpec(memory_space=pltpu.SMEM)

ANY = pl.BlockSpec(memory_space=pl.ANY)

TILES = 3
CONV = 4


def fetch(pairs, sems):
    copies = [pltpu.make_async_copy(src, dst, sems.at[i]) for i, (src, dst) in enumerate(pairs)]
    for copy in copies:
        copy.start()
    for copy in copies:
        copy.wait()


def pack_kernel(
    me_ref, anchor_hbm, target_hbm, state_hbm, conv_hbm, taps_hbm,
    leaving_ref, offset_ref, row_ref, sums_ref,
    anchor_ref, target_ref, state_ref, conv_ref, taps_ref, slot_of, rank_of, source, sems,
):
    fetch(
        [
            (anchor_hbm, anchor_ref),
            (target_hbm, target_ref),
            (conv_hbm, conv_ref),
            (taps_hbm, taps_ref),
            (state_hbm, state_ref),
        ],
        sems,
    )
    slots = state_ref.shape[0]
    peers = leaving_ref.shape[0]
    me = me_ref[0]
    for o in range(peers):
        slot_of[o] = -1
    for s in range(slots):
        slot_of[(target_ref[s] // slots - me + peers) % peers] = s
    rank = jnp.int32(0)
    for k in range(16):
        offset_ref[k] = 0
    for o in range(1, peers):
        slot = slot_of[o]
        rank_of[o] = rank
        offset_ref[rank] = o
        source[rank] = slot
        rank = rank + (slot >= 0).astype(jnp.int32)
    for s in range(slots):
        offset = (me - anchor_ref[s] // slots + peers) % peers
        row_ref[s] = jnp.where(offset == 0, GROUPS + anchor_ref[s] % slots, rank_of[offset])

    old = [conv_ref[i] for i in range(3)]
    taps = [taps_ref[i : i + 1, :] for i in range(3)]
    sums_ref[0] = old[0] * taps[0] + old[1] * taps[1] + old[2] * taps[2]
    sums_ref[1] = old[1] * taps[0] + old[2] * taps[1]
    for d in range(peers):
        for q in range(CONV):
            leaving_ref[d, 2 * TILES + q] = jnp.zeros((4, 128), jnp.float32)
    for k in range(GROUPS):
        slot = source[k]
        for t in range(16):
            tile = 16 * k + t
            rows, lanes = 8 * (t // 8), 128 * (t % 8)
            block = state_ref[slot, rows : rows + 8, lanes : lanes + 128]
            for h in range(2):
                leaving_ref[tile % peers, 2 * (tile // peers) + h] = block[4 * h : 4 * h + 4]
        receiver = (me + offset_ref[k]) % peers
        for i in range(2):
            sums = sums_ref[i, pl.ds(slot, 1), :]
            for c in range(8):
                r = 8 * i + c
                leaving_ref[receiver, 2 * TILES + r // 4, r % 4 : r % 4 + 1, :] = sums[:, 128 * c : 128 * c + 128]


def pack(me, anchor, target, ssm_state, conv_state, conv_weight, peers):
    slots, _, width = ssm_state.shape
    return pl.pallas_call(
        pack_kernel,
        out_shape=(
            jax.ShapeDtypeStruct((peers, 2 * TILES + CONV, 4, 128), jnp.float32),
            jax.ShapeDtypeStruct((16,), jnp.int32),
            jax.ShapeDtypeStruct((16,), jnp.int32),
            jax.ShapeDtypeStruct((2, slots, width), jnp.float32),
        ),
        in_specs=[SMEM] + [ANY] * 5,
        out_specs=(VMEM, SMEM, SMEM, VMEM),
        scratch_shapes=[
            pltpu.SMEM(anchor.shape, jnp.int32),
            pltpu.SMEM(target.shape, jnp.int32),
            pltpu.VMEM(ssm_state.shape, jnp.float32),
            pltpu.VMEM(conv_state.shape, jnp.float32),
            pltpu.VMEM(conv_weight.shape, jnp.float32),
            pltpu.SMEM((peers,), jnp.int32),
            pltpu.SMEM((peers,), jnp.int32),
            pltpu.SMEM((16,), jnp.int32),
            pltpu.SemaphoreType.DMA((5,)),
        ],
        compiler_params=pltpu.CompilerParams(vmem_limit_bytes=56 << 20),
        name="pack",
    )(me, anchor, target, ssm_state, conv_state, conv_weight)


def roll_kernel(me_ref, offset_ref, held_ref, due_ref):
    peers = held_ref.shape[0]
    shifts = [offset_ref[4 * u + me_ref[0] // 16] for u in range(TILES)]

    def body(d, carry):
        for u, shift in enumerate(shifts):
            sender = (d - shift + peers) % peers
            for h in range(2):
                due_ref[d, 2 * u + h] = held_ref[sender, 2 * u + h]
        return carry

    lax.fori_loop(0, peers, body, 0, unroll=8)


def roll(me, offset, held):
    peers = held.shape[0]
    return pl.pallas_call(
        roll_kernel,
        out_shape=jax.ShapeDtypeStruct((peers, 2 * TILES, 4, 128), jnp.float32),
        in_specs=[SMEM, SMEM, VMEM],
        out_specs=VMEM,
        compiler_params=pltpu.CompilerParams(vmem_limit_bytes=32 << 20),
        name="roll",
    )(me, offset, held)


def update_kernel(
    row_hbm, rest_hbm, moved_ref, state_ref, step_ref, x_ref, skip_ref, decay_ref, gate_ref,
    mixed_ref, out_ref,
    row_ref, rest_ref, held, y_ref, sems,
):
    fetch([(row_hbm, row_ref), (rest_hbm, rest_ref)], sems)
    slots, state_size, width = state_ref.shape
    steps = step_ref.shape[0]
    for s in range(slots):
        r = row_ref[s]

        @pl.when(r < GROUPS)
        def _():
            rank = jnp.minimum(r, GROUPS - 1)
            base, group = rank % 4 * 16, rank // 4 * 2
            for t in range(16):
                rows, lanes = 8 * (t // 8), 128 * (t % 8)
                held[s, rows : rows + 8, lanes : lanes + 128] = jnp.concatenate(
                    [moved_ref[base + t, group], moved_ref[base + t, group + 1]]
                )

        @pl.when(r >= GROUPS)
        def _():
            held[s] = state_ref[jnp.maximum(r - GROUPS, 0)]

    for s in range(slots):
        b = [rest_ref[i, :state_size, s : s + 1] for i in range(steps)]
        c = [rest_ref[i, state_size:, s : s + 1] for i in range(steps)]
        for lanes in range(0, width, 128):
            cut = slice(lanes, lanes + 128)
            state = held[s, :, cut]
            decay = decay_ref[:, cut]
            for i in range(steps):
                step = step_ref[i, s : s + 1, cut]
                state = jnp.exp(-step * decay) * state + (step * x_ref[i, s : s + 1, cut]) * b[i]
                y_ref[s, i : i + 1, cut] = jnp.sum(c[i] * state, axis=0, keepdims=True)
            out_ref[s, :, cut] = state
        gate = gate_ref[s].astype(jnp.float32)
        mixed_ref[s] = ((y_ref[s] + skip_ref[s]) * jax.nn.silu(gate)).astype(mixed_ref.dtype)


def update(row, rest, moved, state, step, x, skip, decay, gate):
    return pl.pallas_call(
        update_kernel,
        out_shape=(
            jax.ShapeDtypeStruct(gate.shape, jnp.bfloat16),
            jax.ShapeDtypeStruct(state.shape, jnp.float32),
        ),
        in_specs=[ANY, ANY] + [VMEM] * 7,
        out_specs=(VMEM, VMEM),
        scratch_shapes=[
            pltpu.SMEM(row.shape, jnp.int32),
            pltpu.VMEM(rest.shape, jnp.float32),
            pltpu.VMEM(state.shape, jnp.float32),
            pltpu.VMEM(gate.shape, jnp.float32),
            pltpu.SemaphoreType.DMA((2,)),
        ],
        compiler_params=pltpu.CompilerParams(vmem_limit_bytes=32 << 20),
        name="update",
    )(row, rest, moved, state, step, x, skip, decay, gate)


def exchange(chunks):
    return lax.all_to_all(chunks, "inst", 0, 0)


def sum_over_tp(part):
    half = part.shape[0] // 2
    size = lax.axis_size("tp")
    first = lax.axis_index("tp") % 2 == 0

    def swap(array, bit):
        return lax.ppermute(array, "tp", [(i, i ^ bit) for i in range(size)])

    mine = jnp.where(first, part[:half], part[half:]) + swap(jnp.where(first, part[half:], part[:half]), 1)
    bit = 2
    while bit < size:
        mine = mine + swap(mine, bit)
        bit *= 2
    other = swap(mine, 1)
    return jnp.concatenate([jnp.where(first, mine, other), jnp.where(first, other, mine)])


def local(
    anchor,
    target,
    ssm_state,
    conv_state,
    x_in,
    gate_in,
    conv_weight,
    x_weight,
    dt_weight,
    dt_bias,
    a_log,
    d_skip,
    dt_gain,
):
    slots, state_size, width = ssm_state.shape
    steps = x_in.shape[1]
    taps = conv_weight.shape[0]
    peers = lax.axis_size("inst")
    me = lax.axis_index("inst").astype(jnp.int32).reshape(1)

    leaving, offset, row, sums = pack(me, anchor, target, ssm_state, conv_state.transpose(1, 0, 2), conv_weight, peers)
    spread = exchange(leaving)
    moved = exchange(roll(me, offset, spread))

    came = spread[:, 2 * TILES :].reshape(peers, steps, width)
    partial = jnp.where(
        (anchor // slots == me)[:, None, None],
        jnp.take(sums.transpose(1, 0, 2), anchor % slots, axis=0),
        jnp.take(came, anchor // slots, axis=0),
    )
    x_values = x_in.astype(jnp.float32)
    conved = []
    for i in range(steps):
        window = partial[:, i] + jnp.sum(x_values[:, : i + 1] * conv_weight[None, taps - 1 - i :], axis=1)
        conved.append(jax.nn.silu(window).astype(jnp.bfloat16))
    conved = jnp.concatenate(conved, axis=0)
    totals = sum_over_tp(jnp.dot(conved, x_weight, preferred_element_type=jnp.float32))
    dt_part = totals[:, :DTR]
    inv_rms = lax.rsqrt(jnp.mean(dt_part * dt_part, axis=-1, keepdims=True) + 1e-06)
    dt_low = (dt_part * inv_rms * dt_gain).astype(jnp.bfloat16)
    step_size = jax.nn.softplus(jnp.dot(dt_low, dt_weight, preferred_element_type=jnp.float32) + dt_bias)
    rest = totals[:, DTR:].reshape(steps, slots, 2 * state_size).transpose(0, 2, 1)
    x_rows = conved.astype(jnp.float32).reshape(steps, slots, width)
    return update(
        row,
        rest,
        moved,
        ssm_state,
        step_size.reshape(steps, slots, width),
        x_rows,
        (d_skip * x_rows).transpose(1, 0, 2),
        jnp.exp(a_log),
        gate_in,
    )


def solution(mesh):
    return jax.shard_map(
        local,
        mesh=mesh,
        in_specs=(
            P("inst"),
            P("inst"),
            P("inst", None, "tp"),
            P("inst", None, "tp"),
            P("inst", None, "tp"),
            P("inst", None, "tp"),
            P(None, "tp"),
            P("tp", None),
            P(None, "tp"),
            P("tp"),
            P(None, "tp"),
            P("tp"),
            P(),
        ),
        out_specs=(P("inst", None, "tp"), P("inst", None, "tp")),
        check_vma=False,
    )
```

```python
import jax
import jax.numpy as jnp
from jax import lax
from jax.experimental import pallas as pl
from jax.experimental.pallas import tpu as pltpu
from jax.sharding import PartitionSpec as P

DTR = 512
GROUPS = 12
VMEM = pl.BlockSpec(memory_space=pltpu.VMEM)
SMEM = pl.BlockSpec(memory_space=pltpu.SMEM)

ANY = pl.BlockSpec(memory_space=pl.ANY)

TILES = 3
CONV = 4


def begin(pairs, sems):
    copies = [pltpu.make_async_copy(src, dst, sems.at[i]) for i, (src, dst) in enumerate(pairs)]
    for copy in copies:
        copy.start()
    return copies


def pack_kernel(
    me_ref, anchor_hbm, target_hbm, state_hbm, conv_hbm, taps_hbm,
    leaving_ref, offset_ref, row_ref, sums_ref,
    anchor_ref, target_ref, state_ref, conv_ref, taps_ref, slot_of, rank_of, source, sems,
):
    copies = begin(
        [
            (anchor_hbm, anchor_ref),
            (target_hbm, target_ref),
            (conv_hbm, conv_ref),
            (taps_hbm, taps_ref),
            (state_hbm, state_ref),
        ],
        sems,
    )
    slots = state_ref.shape[0]
    peers = leaving_ref.shape[0]
    me = me_ref[0]
    for d in range(peers):
        for q in range(CONV):
            leaving_ref[d, 2 * TILES + q] = jnp.zeros((4, 128), jnp.float32)
    for o in range(peers):
        slot_of[o] = -1
    for copy in copies[:2]:
        copy.wait()
    for s in range(slots):
        slot_of[(target_ref[s] // slots - me + peers) % peers] = s
    rank = jnp.int32(0)
    for k in range(16):
        offset_ref[k] = 0
    for o in range(1, peers):
        slot = slot_of[o]
        rank_of[o] = rank
        offset_ref[rank] = o
        source[rank] = slot
        rank = rank + (slot >= 0).astype(jnp.int32)
    for s in range(slots):
        offset = (me - anchor_ref[s] // slots + peers) % peers
        row_ref[s] = jnp.where(offset == 0, GROUPS + anchor_ref[s] % slots, rank_of[offset])

    for copy in copies[2:4]:
        copy.wait()
    old = [conv_ref[i] for i in range(3)]
    taps = [taps_ref[i : i + 1, :] for i in range(3)]
    sums_ref[0] = old[0] * taps[0] + old[1] * taps[1] + old[2] * taps[2]
    sums_ref[1] = old[1] * taps[0] + old[2] * taps[1]
    copies[4].wait()
    for k in range(GROUPS):
        slot = source[k]
        for t in range(16):
            tile = 16 * k + t
            rows, lanes = 8 * (t // 8), 128 * (t % 8)
            block = state_ref[slot, rows : rows + 8, lanes : lanes + 128]
            for h in range(2):
                leaving_ref[tile % peers, 2 * (tile // peers) + h] = block[4 * h : 4 * h + 4]
        receiver = (me + offset_ref[k]) % peers
        for i in range(2):
            sums = sums_ref[i, pl.ds(slot, 1), :]
            for c in range(8):
                r = 8 * i + c
                leaving_ref[receiver, 2 * TILES + r // 4, r % 4 : r % 4 + 1, :] = sums[:, 128 * c : 128 * c + 128]


def pack(me, anchor, target, ssm_state, conv_state, conv_weight, peers):
    slots, _, width = ssm_state.shape
    return pl.pallas_call(
        pack_kernel,
        out_shape=(
            jax.ShapeDtypeStruct((peers, 2 * TILES + CONV, 4, 128), jnp.float32),
            jax.ShapeDtypeStruct((16,), jnp.int32),
            jax.ShapeDtypeStruct((16,), jnp.int32),
            jax.ShapeDtypeStruct((2, slots, width), jnp.float32),
        ),
        in_specs=[SMEM] + [ANY] * 5,
        out_specs=(VMEM, SMEM, SMEM, VMEM),
        scratch_shapes=[
            pltpu.SMEM(anchor.shape, jnp.int32),
            pltpu.SMEM(target.shape, jnp.int32),
            pltpu.VMEM(ssm_state.shape, jnp.float32),
            pltpu.VMEM(conv_state.shape, jnp.float32),
            pltpu.VMEM(conv_weight.shape, jnp.float32),
            pltpu.SMEM((peers,), jnp.int32),
            pltpu.SMEM((peers,), jnp.int32),
            pltpu.SMEM((16,), jnp.int32),
            pltpu.SemaphoreType.DMA((5,)),
        ],
        compiler_params=pltpu.CompilerParams(vmem_limit_bytes=56 << 20),
        name="pack",
    )(me, anchor, target, ssm_state, conv_state, conv_weight)


def roll_kernel(me_ref, offset_ref, held_ref, due_ref):
    peers = held_ref.shape[0]
    shifts = [offset_ref[4 * u + me_ref[0] // 16] for u in range(TILES)]

    def body(d, carry):
        for u, shift in enumerate(shifts):
            sender = (d - shift + peers) % peers
            for h in range(2):
                due_ref[d, 2 * u + h] = held_ref[sender, 2 * u + h]
        return carry

    lax.fori_loop(0, peers, body, 0, unroll=8)


def roll(me, offset, held):
    peers = held.shape[0]
    return pl.pallas_call(
        roll_kernel,
        out_shape=jax.ShapeDtypeStruct((peers, 2 * TILES, 4, 128), jnp.float32),
        in_specs=[SMEM, SMEM, VMEM],
        out_specs=VMEM,
        compiler_params=pltpu.CompilerParams(vmem_limit_bytes=32 << 20),
        name="roll",
    )(me, offset, held)


def plan_kernel(step_ref, x_ref, rest_ref, skip_ref, decay_ref, p_ref, q_ref, g_ref, y_ref):
    steps, slots, width = step_ref.shape
    state_size = decay_ref.shape[0]
    for s in range(slots):
        b = [rest_ref[i, :state_size, s : s + 1] for i in range(steps)]
        c = [rest_ref[i, state_size:, s : s + 1] for i in range(steps)]
        for lanes in range(0, width, 128):
            cut = slice(lanes, lanes + 128)
            decay = decay_ref[:, cut]
            p, q = None, None
            for i in range(steps):
                step = step_ref[i, s : s + 1, cut]
                x = x_ref[i, s : s + 1, cut]
                kept = jnp.exp(-step * decay)
                added = (step * x) * b[i]
                p, q = (kept, added) if p is None else (kept * p, kept * q + added)
                g_ref[i, s, :, cut] = c[i] * p
                y_ref[s, i : i + 1, cut] = jnp.sum(c[i] * q, axis=0, keepdims=True) + skip_ref[:, cut] * x
            p_ref[s, :, cut] = p
            q_ref[s, :, cut] = q


def plan(step, x, rest, skip, decay):
    steps, slots, width = step.shape
    whole = jax.ShapeDtypeStruct((slots, *decay.shape), jnp.float32)
    return pl.pallas_call(
        plan_kernel,
        out_shape=(
            whole,
            whole,
            jax.ShapeDtypeStruct((steps, *whole.shape), jnp.float32),
            jax.ShapeDtypeStruct((slots, steps, width), jnp.float32),
        ),
        in_specs=[VMEM] * 5,
        out_specs=(VMEM,) * 4,
        compiler_params=pltpu.CompilerParams(vmem_limit_bytes=32 << 20),
        name="plan",
    )(step, x, rest, skip, decay)


def update_kernel(row_hbm, moved_ref, state_ref, p_ref, q_ref, g_ref, plus_ref, gate_ref, mixed_ref, out_ref, row_ref, y_ref, sems):
    for copy in begin([(row_hbm, row_ref)], sems):
        copy.wait()
    slots, state_size, width = state_ref.shape
    steps = g_ref.shape[0]
    for s in range(slots):
        r = row_ref[s]

        def advance(get):
            for t in range(width // 128):
                cut = slice(128 * t, 128 * t + 128)
                sums = [0.0] * steps
                for n in range(state_size // 8):
                    rows = slice(8 * n, 8 * n + 8)
                    state = get(n, t)
                    out_ref[s, rows, cut] = p_ref[s, rows, cut] * state + q_ref[s, rows, cut]
                    for i in range(steps):
                        sums[i] = sums[i] + g_ref[i, s, rows, cut] * state
                for i in range(steps):
                    y_ref[s, i : i + 1, cut] = jnp.sum(sums[i], axis=0, keepdims=True)

        @pl.when(r < GROUPS)
        def _():
            rank = jnp.minimum(r, GROUPS - 1)
            base, group = rank % 4 * 16, rank // 4 * 2
            advance(
                lambda n, t: jnp.concatenate(
                    [moved_ref[base + 8 * n + t, group], moved_ref[base + 8 * n + t, group + 1]]
                )
            )

        @pl.when(r >= GROUPS)
        def _():
            slot = jnp.maximum(r - GROUPS, 0)
            advance(lambda n, t: state_ref[slot, 8 * n : 8 * n + 8, 128 * t : 128 * t + 128])

        gate = gate_ref[s].astype(jnp.float32)
        mixed_ref[s] = ((y_ref[s] + plus_ref[s]) * jax.nn.silu(gate)).astype(mixed_ref.dtype)


def update(row, moved, state, p, q, g, plus, gate):
    return pl.pallas_call(
        update_kernel,
        out_shape=(
            jax.ShapeDtypeStruct(gate.shape, jnp.bfloat16),
            jax.ShapeDtypeStruct(state.shape, jnp.float32),
        ),
        in_specs=[ANY] + [VMEM] * 7,
        out_specs=(VMEM, VMEM),
        scratch_shapes=[
            pltpu.SMEM(row.shape, jnp.int32),
            pltpu.VMEM(gate.shape, jnp.float32),
            pltpu.SemaphoreType.DMA((1,)),
        ],
        compiler_params=pltpu.CompilerParams(vmem_limit_bytes=32 << 20),
        name="update",
    )(row, moved, state, p, q, g, plus, gate)


def exchange(chunks):
    return lax.all_to_all(chunks, "inst", 0, 0)


def sum_over_tp(part):
    size = lax.axis_size("tp")
    bit = 1
    while bit < size:
        part = part + lax.ppermute(part, "tp", [(i, i ^ bit) for i in range(size)])
        bit *= 2
    return part


def local(
    anchor,
    target,
    ssm_state,
    conv_state,
    x_in,
    gate_in,
    conv_weight,
    x_weight,
    dt_weight,
    dt_bias,
    a_log,
    d_skip,
    dt_gain,
):
    slots, state_size, width = ssm_state.shape
    steps = x_in.shape[1]
    taps = conv_weight.shape[0]
    peers = lax.axis_size("inst")
    me = lax.axis_index("inst").astype(jnp.int32).reshape(1)

    leaving, offset, row, sums = pack(me, anchor, target, ssm_state, conv_state.transpose(1, 0, 2), conv_weight, peers)
    spread = exchange(leaving)
    moved = exchange(roll(me, offset, spread))

    came = spread[:, 2 * TILES :].reshape(peers, steps, width)
    partial = jnp.where(
        (anchor // slots == me)[:, None, None],
        jnp.take(sums.transpose(1, 0, 2), anchor % slots, axis=0),
        jnp.take(came, anchor // slots, axis=0),
    )
    x_values = x_in.astype(jnp.float32)
    conved = []
    for i in range(steps):
        window = partial[:, i] + jnp.sum(x_values[:, : i + 1] * conv_weight[None, taps - 1 - i :], axis=1)
        conved.append(jax.nn.silu(window).astype(jnp.bfloat16))
    conved = jnp.concatenate(conved, axis=0)
    totals = sum_over_tp(jnp.dot(conved, x_weight, preferred_element_type=jnp.float32))
    dt_part = totals[:, :DTR]
    inv_rms = lax.rsqrt(jnp.mean(dt_part * dt_part, axis=-1, keepdims=True) + 1e-06)
    dt_low = (dt_part * inv_rms * dt_gain).astype(jnp.bfloat16)
    step_size = jax.nn.softplus(jnp.dot(dt_low, dt_weight, preferred_element_type=jnp.float32) + dt_bias)
    rest = totals[:, DTR:].reshape(steps, slots, 2 * state_size).transpose(0, 2, 1)
    p, q, g, plus = plan(
        step_size.reshape(steps, slots, width),
        conved.astype(jnp.float32).reshape(steps, slots, width),
        rest,
        d_skip.reshape(1, width),
        jnp.exp(a_log),
    )
    return update(row, moved, ssm_state, p, q, g, plus, gate_in)


def solution(mesh):
    return jax.shard_map(
        local,
        mesh=mesh,
        in_specs=(
            P("inst"),
            P("inst"),
            P("inst", None, "tp"),
            P("inst", None, "tp"),
            P("inst", None, "tp"),
            P("inst", None, "tp"),
            P(None, "tp"),
            P("tp", None),
            P(None, "tp"),
            P("tp"),
            P(None, "tp"),
            P("tp"),
            P(),
        ),
        out_specs=(P("inst", None, "tp"), P("inst", None, "tp")),
        check_vma=False,
    )
```

```python
import jax
import jax.numpy as jnp
from jax import lax
from jax.experimental import pallas as pl
from jax.experimental.pallas import tpu as pltpu
from jax.sharding import PartitionSpec as P

DTR = 512
GROUPS = 12
VMEM = pl.BlockSpec(memory_space=pltpu.VMEM)
SMEM = pl.BlockSpec(memory_space=pltpu.SMEM)

ANY = pl.BlockSpec(memory_space=pl.ANY)

TILES = 3
CONV = 4


def begin(pairs, sems):
    copies = [pltpu.make_async_copy(src, dst, sems.at[i]) for i, (src, dst) in enumerate(pairs)]
    for copy in copies:
        copy.start()
    return copies


def pack_kernel(
    me_ref, anchor_hbm, target_hbm, state_hbm, conv_hbm, taps_hbm,
    leaving_ref, offset_ref, row_ref, sums_ref,
    anchor_ref, target_ref, state_ref, conv_ref, taps_ref, slot_of, rank_of, source, sems,
):
    copies = begin(
        [
            (anchor_hbm, anchor_ref),
            (target_hbm, target_ref),
            (conv_hbm, conv_ref),
            (taps_hbm, taps_ref),
            (state_hbm, state_ref),
        ],
        sems,
    )
    slots = state_ref.shape[0]
    peers = leaving_ref.shape[0]
    me = me_ref[0]
    for d in range(peers):
        for q in range(CONV):
            leaving_ref[d, 2 * TILES + q] = jnp.zeros((4, 128), jnp.float32)
    for o in range(peers):
        slot_of[o] = -1
    for copy in copies[:2]:
        copy.wait()
    for s in range(slots):
        slot_of[(target_ref[s] // slots - me + peers) % peers] = s
    rank = jnp.int32(0)
    for k in range(16):
        offset_ref[k] = 0
    for o in range(1, peers):
        slot = slot_of[o]
        rank_of[o] = rank
        offset_ref[rank] = o
        source[rank] = slot
        rank = rank + (slot >= 0).astype(jnp.int32)
    for s in range(slots):
        offset = (me - anchor_ref[s] // slots + peers) % peers
        row_ref[s] = jnp.where(offset == 0, GROUPS + anchor_ref[s] % slots, rank_of[offset])

    for copy in copies[2:4]:
        copy.wait()
    old = [conv_ref[i] for i in range(3)]
    taps = [taps_ref[i : i + 1, :] for i in range(3)]
    sums_ref[0] = old[0] * taps[0] + old[1] * taps[1] + old[2] * taps[2]
    sums_ref[1] = old[1] * taps[0] + old[2] * taps[1]
    copies[4].wait()
    for k in range(GROUPS):
        slot = source[k]
        for t in range(16):
            tile = 16 * k + t
            rows, lanes = 8 * (t // 8), 128 * (t % 8)
            block = state_ref[slot, rows : rows + 8, lanes : lanes + 128]
            for h in range(2):
                leaving_ref[tile % peers, 2 * (tile // peers) + h] = block[4 * h : 4 * h + 4]
        receiver = (me + offset_ref[k]) % peers
        for i in range(2):
            sums = sums_ref[i, pl.ds(slot, 1), :]
            for c in range(8):
                r = 8 * i + c
                leaving_ref[receiver, 2 * TILES + r // 4, r % 4 : r % 4 + 1, :] = sums[:, 128 * c : 128 * c + 128]


def pack(me, anchor, target, ssm_state, conv_state, conv_weight, peers):
    slots, _, width = ssm_state.shape
    return pl.pallas_call(
        pack_kernel,
        out_shape=(
            jax.ShapeDtypeStruct((peers, 2 * TILES + CONV, 4, 128), jnp.float32),
            jax.ShapeDtypeStruct((16,), jnp.int32),
            jax.ShapeDtypeStruct((16,), jnp.int32),
            jax.ShapeDtypeStruct((2, slots, width), jnp.float32),
        ),
        in_specs=[SMEM] + [ANY] * 5,
        out_specs=(VMEM, SMEM, SMEM, VMEM),
        scratch_shapes=[
            pltpu.SMEM(anchor.shape, jnp.int32),
            pltpu.SMEM(target.shape, jnp.int32),
            pltpu.VMEM(ssm_state.shape, jnp.float32),
            pltpu.VMEM(conv_state.shape, jnp.float32),
            pltpu.VMEM(conv_weight.shape, jnp.float32),
            pltpu.SMEM((peers,), jnp.int32),
            pltpu.SMEM((peers,), jnp.int32),
            pltpu.SMEM((16,), jnp.int32),
            pltpu.SemaphoreType.DMA((5,)),
        ],
        compiler_params=pltpu.CompilerParams(vmem_limit_bytes=56 << 20),
        name="pack",
    )(me, anchor, target, ssm_state, conv_state, conv_weight)


def roll_kernel(me_ref, offset_ref, held_ref, due_ref):
    peers = held_ref.shape[0]
    shifts = [offset_ref[4 * u + me_ref[0] // 16] for u in range(TILES)]

    def body(d, carry):
        for u, shift in enumerate(shifts):
            sender = (d - shift + peers) % peers
            for h in range(2):
                due_ref[d, 2 * u + h] = held_ref[sender, 2 * u + h]
        return carry

    lax.fori_loop(0, peers, body, 0, unroll=8)


def roll(me, offset, held):
    peers = held.shape[0]
    return pl.pallas_call(
        roll_kernel,
        out_shape=jax.ShapeDtypeStruct((peers, 2 * TILES, 4, 128), jnp.float32),
        in_specs=[SMEM, SMEM, VMEM],
        out_specs=VMEM,
        compiler_params=pltpu.CompilerParams(vmem_limit_bytes=12 << 20),
        name="roll",
    )(me, offset, held)


def plan_kernel(step_ref, x_ref, rest_ref, skip_ref, decay_ref, p_ref, q_ref, g_ref, y_ref):
    steps, slots, width = step_ref.shape
    state_size = decay_ref.shape[0]
    for s in range(slots):
        b = [rest_ref[i, :state_size, s : s + 1] for i in range(steps)]
        c = [rest_ref[i, state_size:, s : s + 1] for i in range(steps)]
        for lanes in range(0, width, 128):
            cut = slice(lanes, lanes + 128)
            decay = decay_ref[:, cut]
            p, q = None, None
            for i in range(steps):
                step = step_ref[i, s : s + 1, cut]
                x = x_ref[i, s : s + 1, cut]
                kept = jnp.exp(-step * decay)
                added = (step * x) * b[i]
                p, q = (kept, added) if p is None else (kept * p, kept * q + added)
                g_ref[i, s, :, cut] = c[i] * p
                y_ref[s, i : i + 1, cut] = jnp.sum(c[i] * q, axis=0, keepdims=True) + skip_ref[:, cut] * x
            p_ref[s, :, cut] = p
            q_ref[s, :, cut] = q


def plan(step, x, rest, skip, decay):
    steps, slots, width = step.shape
    whole = jax.ShapeDtypeStruct((slots, *decay.shape), jnp.float32)
    return pl.pallas_call(
        plan_kernel,
        out_shape=(
            whole,
            whole,
            jax.ShapeDtypeStruct((steps, *whole.shape), jnp.float32),
            jax.ShapeDtypeStruct((slots, steps, width), jnp.float32),
        ),
        in_specs=[VMEM] * 5,
        out_specs=(VMEM,) * 4,
        compiler_params=pltpu.CompilerParams(vmem_limit_bytes=12 << 20),
        name="plan",
    )(step, x, rest, skip, decay)


def update_kernel(row_hbm, moved_ref, state_ref, p_ref, q_ref, g_ref, plus_ref, gate_ref, mixed_ref, out_ref, row_ref, y_ref, sems):
    for copy in begin([(row_hbm, row_ref)], sems):
        copy.wait()
    slots, state_size, width = state_ref.shape
    steps = g_ref.shape[0]
    for s in range(slots):
        r = row_ref[s]

        def advance(get):
            for t in range(width // 128):
                cut = slice(128 * t, 128 * t + 128)
                sums = [0.0] * steps
                for n in range(state_size // 8):
                    rows = slice(8 * n, 8 * n + 8)
                    state = get(n, t)
                    out_ref[s, rows, cut] = p_ref[s, rows, cut] * state + q_ref[s, rows, cut]
                    for i in range(steps):
                        sums[i] = sums[i] + g_ref[i, s, rows, cut] * state
                for i in range(steps):
                    y_ref[s, i : i + 1, cut] = jnp.sum(sums[i], axis=0, keepdims=True)

        @pl.when(r < GROUPS)
        def _():
            rank = jnp.minimum(r, GROUPS - 1)
            base, group = rank % 4 * 16, rank // 4 * 2
            advance(
                lambda n, t: jnp.concatenate(
                    [moved_ref[base + 8 * n + t, group], moved_ref[base + 8 * n + t, group + 1]]
                )
            )

        @pl.when(r >= GROUPS)
        def _():
            slot = jnp.maximum(r - GROUPS, 0)
            advance(lambda n, t: state_ref[slot, 8 * n : 8 * n + 8, 128 * t : 128 * t + 128])

        gate = gate_ref[s].astype(jnp.float32)
        mixed_ref[s] = ((y_ref[s] + plus_ref[s]) * jax.nn.silu(gate)).astype(mixed_ref.dtype)


def update(row, moved, state, p, q, g, plus, gate):
    return pl.pallas_call(
        update_kernel,
        out_shape=(
            jax.ShapeDtypeStruct(gate.shape, jnp.bfloat16),
            jax.ShapeDtypeStruct(state.shape, jnp.float32),
        ),
        in_specs=[ANY] + [VMEM] * 7,
        out_specs=(VMEM, VMEM),
        scratch_shapes=[
            pltpu.SMEM(row.shape, jnp.int32),
            pltpu.VMEM(gate.shape, jnp.float32),
            pltpu.SemaphoreType.DMA((1,)),
        ],
        compiler_params=pltpu.CompilerParams(vmem_limit_bytes=12 << 20),
        name="update",
    )(row, moved, state, p, q, g, plus, gate)


def exchange(chunks):
    return lax.all_to_all(chunks, "inst", 0, 0)


def sum_over_tp(part):
    size = lax.axis_size("tp")
    bit = 1
    while bit < size:
        part = part + lax.ppermute(part, "tp", [(i, i ^ bit) for i in range(size)])
        bit *= 2
    return part


def local(
    anchor,
    target,
    ssm_state,
    conv_state,
    x_in,
    gate_in,
    conv_weight,
    x_weight,
    dt_weight,
    dt_bias,
    a_log,
    d_skip,
    dt_gain,
):
    slots, state_size, width = ssm_state.shape
    steps = x_in.shape[1]
    taps = conv_weight.shape[0]
    peers = lax.axis_size("inst")
    me = lax.axis_index("inst").astype(jnp.int32).reshape(1)

    leaving, offset, row, sums = pack(me, anchor, target, ssm_state, conv_state.transpose(1, 0, 2), conv_weight, peers)
    spread = exchange(leaving)
    moved = exchange(roll(me, offset, spread))

    came = spread[:, 2 * TILES :].reshape(peers, steps, width)
    partial = jnp.where(
        (anchor // slots == me)[:, None, None],
        jnp.take(sums.transpose(1, 0, 2), anchor % slots, axis=0),
        jnp.take(came, anchor // slots, axis=0),
    )
    x_values = x_in.astype(jnp.float32)
    conved = []
    for i in range(steps):
        window = partial[:, i] + jnp.sum(x_values[:, : i + 1] * conv_weight[None, taps - 1 - i :], axis=1)
        conved.append(jax.nn.silu(window).astype(jnp.bfloat16))
    conved = jnp.concatenate(conved, axis=0)
    totals = sum_over_tp(jnp.dot(conved, x_weight, preferred_element_type=jnp.float32))
    dt_part = totals[:, :DTR]
    inv_rms = lax.rsqrt(jnp.mean(dt_part * dt_part, axis=-1, keepdims=True) + 1e-06)
    dt_low = (dt_part * inv_rms * dt_gain).astype(jnp.bfloat16)
    step_size = jax.nn.softplus(jnp.dot(dt_low, dt_weight, preferred_element_type=jnp.float32) + dt_bias)
    rest = totals[:, DTR:].reshape(steps, slots, 2 * state_size).transpose(0, 2, 1)
    p, q, g, plus = plan(
        step_size.reshape(steps, slots, width),
        conved.astype(jnp.float32).reshape(steps, slots, width),
        rest,
        d_skip.reshape(1, width),
        jnp.exp(a_log),
    )
    return update(row, moved, ssm_state, p, q, g, plus, gate_in)


def solution(mesh):
    return jax.shard_map(
        local,
        mesh=mesh,
        in_specs=(
            P("inst"),
            P("inst"),
            P("inst", None, "tp"),
            P("inst", None, "tp"),
            P("inst", None, "tp"),
            P("inst", None, "tp"),
            P(None, "tp"),
            P("tp", None),
            P(None, "tp"),
            P("tp"),
            P(None, "tp"),
            P("tp"),
            P(),
        ),
        out_specs=(P("inst", None, "tp"), P("inst", None, "tp")),
        check_vma=False,
    )
```

```python
import jax
import jax.numpy as jnp
from jax import lax
from jax.experimental import pallas as pl
from jax.experimental.pallas import tpu as pltpu
from jax.sharding import PartitionSpec as P

DTR = 512
GROUPS = 12
VMEM = pl.BlockSpec(memory_space=pltpu.VMEM)
SMEM = pl.BlockSpec(memory_space=pltpu.SMEM)

ANY = pl.BlockSpec(memory_space=pl.ANY)

TILES = 3
CONV = 4


def begin(pairs, sems):
    copies = [pltpu.make_async_copy(src, dst, sems.at[i]) for i, (src, dst) in enumerate(pairs)]
    for copy in copies:
        copy.start()
    return copies


def pack_kernel(
    me_ref, anchor_hbm, target_hbm, state_hbm, conv_hbm, taps_hbm,
    leaving_ref, offset_ref, row_ref, sums_ref,
    anchor_ref, target_ref, state_ref, conv_ref, taps_ref, slot_of, rank_of, source, sems,
):
    copies = begin(
        [
            (anchor_hbm, anchor_ref),
            (target_hbm, target_ref),
            (conv_hbm, conv_ref),
            (taps_hbm, taps_ref),
            (state_hbm, state_ref),
        ],
        sems,
    )
    slots = state_ref.shape[0]
    peers = leaving_ref.shape[0]
    me = me_ref[0]
    for d in range(peers):
        for q in range(CONV):
            leaving_ref[d, 2 * TILES + q] = jnp.zeros((4, 128), jnp.float32)
    for o in range(peers):
        slot_of[o] = -1
    for copy in copies[:2]:
        copy.wait()
    for s in range(slots):
        slot_of[(target_ref[s] // slots - me + peers) % peers] = s
    rank = jnp.int32(0)
    for k in range(16):
        offset_ref[k] = 0
    for o in range(1, peers):
        slot = slot_of[o]
        rank_of[o] = rank
        offset_ref[rank] = o
        source[rank] = slot
        rank = rank + (slot >= 0).astype(jnp.int32)
    for s in range(slots):
        offset = (me - anchor_ref[s] // slots + peers) % peers
        row_ref[s] = jnp.where(offset == 0, GROUPS + anchor_ref[s] % slots, rank_of[offset])

    for copy in copies[2:4]:
        copy.wait()
    old = [conv_ref[i] for i in range(3)]
    taps = [taps_ref[i : i + 1, :] for i in range(3)]
    sums_ref[0] = old[0] * taps[0] + old[1] * taps[1] + old[2] * taps[2]
    sums_ref[1] = old[1] * taps[0] + old[2] * taps[1]
    copies[4].wait()
    for k in range(GROUPS):
        slot = source[k]
        for t in range(16):
            tile = 16 * k + t
            rows, lanes = 8 * (t // 8), 128 * (t % 8)
            block = state_ref[slot, rows : rows + 8, lanes : lanes + 128]
            for h in range(2):
                leaving_ref[tile % peers, 2 * (tile // peers) + h] = block[4 * h : 4 * h + 4]
        receiver = (me + offset_ref[k]) % peers
        for i in range(2):
            sums = sums_ref[i, pl.ds(slot, 1), :]
            for c in range(8):
                r = 8 * i + c
                leaving_ref[receiver, 2 * TILES + r // 4, r % 4 : r % 4 + 1, :] = sums[:, 128 * c : 128 * c + 128]


def pack(me, anchor, target, ssm_state, conv_state, conv_weight, peers):
    slots, _, width = ssm_state.shape
    return pl.pallas_call(
        pack_kernel,
        out_shape=(
            jax.ShapeDtypeStruct((peers, 2 * TILES + CONV, 4, 128), jnp.float32),
            jax.ShapeDtypeStruct((16,), jnp.int32),
            jax.ShapeDtypeStruct((16,), jnp.int32),
            jax.ShapeDtypeStruct((2, slots, width), jnp.float32),
        ),
        in_specs=[SMEM] + [ANY] * 5,
        out_specs=(VMEM, SMEM, SMEM, VMEM),
        scratch_shapes=[
            pltpu.SMEM(anchor.shape, jnp.int32),
            pltpu.SMEM(target.shape, jnp.int32),
            pltpu.VMEM(ssm_state.shape, jnp.float32),
            pltpu.VMEM(conv_state.shape, jnp.float32),
            pltpu.VMEM(conv_weight.shape, jnp.float32),
            pltpu.SMEM((peers,), jnp.int32),
            pltpu.SMEM((peers,), jnp.int32),
            pltpu.SMEM((16,), jnp.int32),
            pltpu.SemaphoreType.DMA((5,)),
        ],
        compiler_params=pltpu.CompilerParams(vmem_limit_bytes=56 << 20),
        name="pack",
    )(me, anchor, target, ssm_state, conv_state, conv_weight)


def roll_kernel(me_ref, offset_ref, held_ref, due_ref):
    peers = held_ref.shape[0]
    shifts = [offset_ref[4 * u + me_ref[0] // 16] for u in range(TILES)]

    def body(d, carry):
        for u, shift in enumerate(shifts):
            sender = (d - shift + peers) % peers
            for h in range(2):
                due_ref[d, 2 * u + h] = held_ref[sender, 2 * u + h]
        return carry

    lax.fori_loop(0, peers, body, 0, unroll=8)


def roll(me, offset, held):
    peers = held.shape[0]
    return pl.pallas_call(
        roll_kernel,
        out_shape=jax.ShapeDtypeStruct((peers, 2 * TILES, 4, 128), jnp.float32),
        in_specs=[SMEM, SMEM, VMEM],
        out_specs=VMEM,
        compiler_params=pltpu.CompilerParams(vmem_limit_bytes=32 << 20),
        name="roll",
    )(me, offset, held)


def update_kernel(
    row_hbm, rest_ref, moved_ref, state_ref, step_ref, x_ref, skip_ref, decay_ref, gate_ref,
    mixed_ref, out_hbm,
    row_ref, out_ref, y_ref, row_sem, out_sems,
):
    for copy in begin([(row_hbm, row_ref)], row_sem):
        copy.wait()
    slots, state_size, width = state_ref.shape
    steps = step_ref.shape[0]
    copies = []
    for s in range(slots):
        r = row_ref[s]
        b = [rest_ref[i, :state_size, s : s + 1] for i in range(steps)]
        c = [rest_ref[i, state_size:, s : s + 1] for i in range(steps)]
        rank = jnp.clip(r, 0, GROUPS - 1)
        base, group = rank % 4 * 16, rank // 4 * 2
        slot = jnp.clip(r - GROUPS, 0, slots - 1)
        for t in range(width // 128):
            cut = slice(128 * t, 128 * t + 128)
            came = [moved_ref[base + 8 * n + t, group + h] for n in range(2) for h in range(2)]
            state = jnp.where(r < GROUPS, jnp.concatenate(came), state_ref[slot, :, cut])
            decay = decay_ref[:, cut]
            for i in range(steps):
                step = step_ref[i, s : s + 1, cut]
                state = jnp.exp(-step * decay) * state + (step * x_ref[i, s : s + 1, cut]) * b[i]
                y_ref[s, i : i + 1, cut] = jnp.sum(c[i] * state, axis=0, keepdims=True)
            out_ref[s, :, cut] = state
        copies.append(pltpu.make_async_copy(out_ref.at[s], out_hbm.at[s], out_sems.at[s]))
        copies[-1].start()
        gate = gate_ref[s].astype(jnp.float32)
        mixed_ref[s] = ((y_ref[s] + skip_ref[s]) * jax.nn.silu(gate)).astype(mixed_ref.dtype)
    for copy in copies:
        copy.wait()


def update(row, rest, moved, state, step, x, skip, decay, gate):
    return pl.pallas_call(
        update_kernel,
        out_shape=(
            jax.ShapeDtypeStruct(gate.shape, jnp.bfloat16),
            jax.ShapeDtypeStruct(state.shape, jnp.float32),
        ),
        in_specs=[ANY] + [VMEM] * 8,
        out_specs=(VMEM, ANY),
        scratch_shapes=[
            pltpu.SMEM(row.shape, jnp.int32),
            pltpu.VMEM(state.shape, jnp.float32),
            pltpu.VMEM(gate.shape, jnp.float32),
            pltpu.SemaphoreType.DMA((1,)),
            pltpu.SemaphoreType.DMA((state.shape[0],)),
        ],
        compiler_params=pltpu.CompilerParams(vmem_limit_bytes=32 << 20),
        name="update",
    )(row, rest, moved, state, step, x, skip, decay, gate)


def exchange(chunks):
    return lax.all_to_all(chunks, "inst", 0, 0)


def sum_over_tp(part):
    size = lax.axis_size("tp")
    bit = 1
    while bit < size:
        part = part + lax.ppermute(part, "tp", [(i, i ^ bit) for i in range(size)])
        bit *= 2
    return part


def local(
    anchor,
    target,
    ssm_state,
    conv_state,
    x_in,
    gate_in,
    conv_weight,
    x_weight,
    dt_weight,
    dt_bias,
    a_log,
    d_skip,
    dt_gain,
):
    slots, state_size, width = ssm_state.shape
    steps = x_in.shape[1]
    taps = conv_weight.shape[0]
    peers = lax.axis_size("inst")
    me = lax.axis_index("inst").astype(jnp.int32).reshape(1)

    leaving, offset, row, sums = pack(me, anchor, target, ssm_state, conv_state.transpose(1, 0, 2), conv_weight, peers)
    spread = exchange(leaving)
    moved = exchange(roll(me, offset, spread))

    came = spread[:, 2 * TILES :].reshape(peers, steps, width)
    partial = jnp.where(
        (anchor // slots == me)[:, None, None],
        jnp.take(sums.transpose(1, 0, 2), anchor % slots, axis=0),
        jnp.take(came, anchor // slots, axis=0),
    )
    x_values = x_in.astype(jnp.float32)
    conved = []
    for i in range(steps):
        window = partial[:, i] + jnp.sum(x_values[:, : i + 1] * conv_weight[None, taps - 1 - i :], axis=1)
        conved.append(jax.nn.silu(window).astype(jnp.bfloat16))
    conved = jnp.concatenate(conved, axis=0)
    totals = sum_over_tp(jnp.dot(conved, x_weight, preferred_element_type=jnp.float32))
    dt_part = totals[:, :DTR]
    inv_rms = lax.rsqrt(jnp.mean(dt_part * dt_part, axis=-1, keepdims=True) + 1e-06)
    dt_low = (dt_part * inv_rms * dt_gain).astype(jnp.bfloat16)
    step_size = jax.nn.softplus(jnp.dot(dt_low, dt_weight, preferred_element_type=jnp.float32) + dt_bias)
    rest = totals[:, DTR:].reshape(steps, slots, 2 * state_size).transpose(0, 2, 1)
    x_rows = conved.astype(jnp.float32).reshape(steps, slots, width)
    return update(
        row,
        rest,
        moved,
        ssm_state,
        step_size.reshape(steps, slots, width),
        x_rows,
        (d_skip * x_rows).transpose(1, 0, 2),
        jnp.exp(a_log),
        gate_in,
    )


def solution(mesh):
    return jax.shard_map(
        local,
        mesh=mesh,
        in_specs=(
            P("inst"),
            P("inst"),
            P("inst", None, "tp"),
            P("inst", None, "tp"),
            P("inst", None, "tp"),
            P("inst", None, "tp"),
            P(None, "tp"),
            P("tp", None),
            P(None, "tp"),
            P("tp"),
            P(None, "tp"),
            P("tp"),
            P(),
        ),
        out_specs=(P("inst", None, "tp"), P("inst", None, "tp")),
        check_vma=False,
    )
```

```python
import jax
import jax.numpy as jnp
from jax import lax
from jax.experimental import pallas as pl
from jax.experimental.pallas import tpu as pltpu
from jax.sharding import PartitionSpec as P

DTR = 512
GROUPS = 12
VMEM = pl.BlockSpec(memory_space=pltpu.VMEM)
SMEM = pl.BlockSpec(memory_space=pltpu.SMEM)

ANY = pl.BlockSpec(memory_space=pl.ANY)

TILES = 3
CONV = 4


def begin(pairs, sems):
    copies = [pltpu.make_async_copy(src, dst, sems.at[i]) for i, (src, dst) in enumerate(pairs)]
    for copy in copies:
        copy.start()
    return copies


def pack_kernel(
    me_ref, anchor_hbm, target_hbm, state_hbm, conv_hbm, taps_hbm,
    leaving_hbm, offset_ref, row_ref, sums_ref,
    leaving_ref, anchor_ref, target_ref, state_ref, conv_ref, taps_ref, slot_of, rank_of, source, sems, out_sems,
):
    copies = begin(
        [
            (anchor_hbm, anchor_ref),
            (target_hbm, target_ref),
            (conv_hbm, conv_ref),
            (taps_hbm, taps_ref),
            (state_hbm, state_ref),
        ],
        sems,
    )
    slots = state_ref.shape[0]
    peers = leaving_ref.shape[0]
    me = me_ref[0]
    for d in range(peers):
        for q in range(CONV):
            leaving_ref[d, 2 * TILES + q] = jnp.zeros((4, 128), jnp.float32)
    for o in range(peers):
        slot_of[o] = -1
    for copy in copies[:2]:
        copy.wait()
    for s in range(slots):
        slot_of[(target_ref[s] // slots - me + peers) % peers] = s
    rank = jnp.int32(0)
    for k in range(16):
        offset_ref[k] = 0
    for o in range(1, peers):
        slot = slot_of[o]
        rank_of[o] = rank
        offset_ref[rank] = o
        source[rank] = slot
        rank = rank + (slot >= 0).astype(jnp.int32)
    for s in range(slots):
        offset = (me - anchor_ref[s] // slots + peers) % peers
        row_ref[s] = jnp.where(offset == 0, GROUPS + anchor_ref[s] % slots, rank_of[offset])

    for copy in copies[2:4]:
        copy.wait()
    old = [conv_ref[i] for i in range(3)]
    taps = [taps_ref[i : i + 1, :] for i in range(3)]
    sums_ref[0] = old[0] * taps[0] + old[1] * taps[1] + old[2] * taps[2]
    sums_ref[1] = old[1] * taps[0] + old[2] * taps[1]
    leaving = []

    def send(low, high):
        part = slice(low, high)
        leaving.append(
            pltpu.make_async_copy(leaving_ref.at[:, part], leaving_hbm.at[:, part], out_sems.at[len(leaving)])
        )
        leaving[-1].start()

    for k in range(GROUPS):
        receiver = (me + offset_ref[k]) % peers
        for i in range(2):
            sums = sums_ref[i, pl.ds(source[k], 1), :]
            for c in range(8):
                r = 8 * i + c
                leaving_ref[receiver, 2 * TILES + r // 4, r % 4 : r % 4 + 1, :] = sums[:, 128 * c : 128 * c + 128]
    send(2 * TILES, 2 * TILES + CONV)
    copies[4].wait()
    for u in range(TILES):
        for k in range(4 * u, 4 * u + 4):
            slot = source[k]
            for t in range(16):
                rows, lanes = 8 * (t // 8), 128 * (t % 8)
                block = state_ref[slot, rows : rows + 8, lanes : lanes + 128]
                for h in range(2):
                    leaving_ref[(16 * k + t) % peers, 2 * u + h] = block[4 * h : 4 * h + 4]
        send(2 * u, 2 * u + 2)
    for copy in leaving:
        copy.wait()


def pack(me, anchor, target, ssm_state, conv_state, conv_weight, peers):
    slots, _, width = ssm_state.shape
    return pl.pallas_call(
        pack_kernel,
        out_shape=(
            jax.ShapeDtypeStruct((peers, 2 * TILES + CONV, 4, 128), jnp.float32),
            jax.ShapeDtypeStruct((16,), jnp.int32),
            jax.ShapeDtypeStruct((16,), jnp.int32),
            jax.ShapeDtypeStruct((2, slots, width), jnp.float32),
        ),
        in_specs=[SMEM] + [ANY] * 5,
        out_specs=(ANY, SMEM, SMEM, VMEM),
        scratch_shapes=[
            pltpu.VMEM((peers, 2 * TILES + CONV, 4, 128), jnp.float32),
            pltpu.SMEM(anchor.shape, jnp.int32),
            pltpu.SMEM(target.shape, jnp.int32),
            pltpu.VMEM(ssm_state.shape, jnp.float32),
            pltpu.VMEM(conv_state.shape, jnp.float32),
            pltpu.VMEM(conv_weight.shape, jnp.float32),
            pltpu.SMEM((peers,), jnp.int32),
            pltpu.SMEM((peers,), jnp.int32),
            pltpu.SMEM((16,), jnp.int32),
            pltpu.SemaphoreType.DMA((5,)),
            pltpu.SemaphoreType.DMA((TILES + 1,)),
        ],
        compiler_params=pltpu.CompilerParams(vmem_limit_bytes=54 << 20),
        name="pack",
    )(me, anchor, target, ssm_state, conv_state, conv_weight)


def roll_kernel(me_ref, offset_ref, held_ref, due_ref):
    peers = held_ref.shape[0]
    shifts = [offset_ref[4 * u + me_ref[0] // 16] for u in range(TILES)]

    def body(d, carry):
        for u, shift in enumerate(shifts):
            sender = (d - shift + peers) % peers
            for h in range(2):
                due_ref[d, 2 * u + h] = held_ref[sender, 2 * u + h]
        return carry

    lax.fori_loop(0, peers, body, 0, unroll=8)


def roll(me, offset, held):
    peers = held.shape[0]
    return pl.pallas_call(
        roll_kernel,
        out_shape=jax.ShapeDtypeStruct((peers, 2 * TILES, 4, 128), jnp.float32),
        in_specs=[SMEM, SMEM, VMEM],
        out_specs=VMEM,
        compiler_params=pltpu.CompilerParams(vmem_limit_bytes=32 << 20),
        name="roll",
    )(me, offset, held)


def update_kernel(
    row_hbm, rest_ref, moved_ref, state_ref, step_ref, x_ref, skip_ref, decay_ref, gate_ref,
    mixed_ref, out_hbm,
    row_ref, out_ref, y_ref, row_sem, out_sems,
):
    for copy in begin([(row_hbm, row_ref)], row_sem):
        copy.wait()
    slots, state_size, width = state_ref.shape
    steps = step_ref.shape[0]
    copies = []
    for s in range(slots):
        r = row_ref[s]
        b = [rest_ref[i, :state_size, s : s + 1] for i in range(steps)]
        c = [rest_ref[i, state_size:, s : s + 1] for i in range(steps)]
        rank = jnp.clip(r, 0, GROUPS - 1)
        base, group = rank % 4 * 16, rank // 4 * 2
        slot = jnp.clip(r - GROUPS, 0, slots - 1)
        for t in range(width // 128):
            cut = slice(128 * t, 128 * t + 128)
            came = [moved_ref[base + 8 * n + t, group + h] for n in range(2) for h in range(2)]
            state = jnp.where(r < GROUPS, jnp.concatenate(came), state_ref[slot, :, cut])
            decay = decay_ref[:, cut]
            for i in range(steps):
                step = step_ref[i, s : s + 1, cut]
                state = jnp.exp(-step * decay) * state + (step * x_ref[i, s : s + 1, cut]) * b[i]
                y_ref[s, i : i + 1, cut] = jnp.sum(c[i] * state, axis=0, keepdims=True)
            out_ref[s, :, cut] = state
        copies.append(pltpu.make_async_copy(out_ref.at[s], out_hbm.at[s], out_sems.at[s]))
        copies[-1].start()
        gate = gate_ref[s].astype(jnp.float32)
        mixed_ref[s] = ((y_ref[s] + skip_ref[s]) * jax.nn.silu(gate)).astype(mixed_ref.dtype)
    for copy in copies:
        copy.wait()


def update(row, rest, moved, state, step, x, skip, decay, gate):
    return pl.pallas_call(
        update_kernel,
        out_shape=(
            jax.ShapeDtypeStruct(gate.shape, jnp.bfloat16),
            jax.ShapeDtypeStruct(state.shape, jnp.float32),
        ),
        in_specs=[ANY] + [VMEM] * 8,
        out_specs=(VMEM, ANY),
        scratch_shapes=[
            pltpu.SMEM(row.shape, jnp.int32),
            pltpu.VMEM(state.shape, jnp.float32),
            pltpu.VMEM(gate.shape, jnp.float32),
            pltpu.SemaphoreType.DMA((1,)),
            pltpu.SemaphoreType.DMA((state.shape[0],)),
        ],
        compiler_params=pltpu.CompilerParams(vmem_limit_bytes=32 << 20),
        name="update",
    )(row, rest, moved, state, step, x, skip, decay, gate)


def exchange(chunks):
    return lax.all_to_all(chunks, "inst", 0, 0)


def sum_over_tp(part):
    size = lax.axis_size("tp")
    bit = 1
    while bit < size:
        part = part + lax.ppermute(part, "tp", [(i, i ^ bit) for i in range(size)])
        bit *= 2
    return part


def local(
    anchor,
    target,
    ssm_state,
    conv_state,
    x_in,
    gate_in,
    conv_weight,
    x_weight,
    dt_weight,
    dt_bias,
    a_log,
    d_skip,
    dt_gain,
):
    slots, state_size, width = ssm_state.shape
    steps = x_in.shape[1]
    taps = conv_weight.shape[0]
    peers = lax.axis_size("inst")
    me = lax.axis_index("inst").astype(jnp.int32).reshape(1)

    leaving, offset, row, sums = pack(me, anchor, target, ssm_state, conv_state.transpose(1, 0, 2), conv_weight, peers)
    spread = exchange(leaving)
    moved = exchange(roll(me, offset, spread))

    came = spread[:, 2 * TILES :].reshape(peers, steps, width)
    partial = jnp.where(
        (anchor // slots == me)[:, None, None],
        jnp.take(sums.transpose(1, 0, 2), anchor % slots, axis=0),
        jnp.take(came, anchor // slots, axis=0),
    )
    x_values = x_in.astype(jnp.float32)
    conved = []
    for i in range(steps):
        window = partial[:, i] + jnp.sum(x_values[:, : i + 1] * conv_weight[None, taps - 1 - i :], axis=1)
        conved.append(jax.nn.silu(window).astype(jnp.bfloat16))
    conved = jnp.concatenate(conved, axis=0)
    totals = sum_over_tp(jnp.dot(conved, x_weight, preferred_element_type=jnp.float32))
    dt_part = totals[:, :DTR]
    inv_rms = lax.rsqrt(jnp.mean(dt_part * dt_part, axis=-1, keepdims=True) + 1e-06)
    dt_low = (dt_part * inv_rms * dt_gain).astype(jnp.bfloat16)
    step_size = jax.nn.softplus(jnp.dot(dt_low, dt_weight, preferred_element_type=jnp.float32) + dt_bias)
    rest = totals[:, DTR:].reshape(steps, slots, 2 * state_size).transpose(0, 2, 1)
    x_rows = conved.astype(jnp.float32).reshape(steps, slots, width)
    return update(
        row,
        rest,
        moved,
        ssm_state,
        step_size.reshape(steps, slots, width),
        x_rows,
        (d_skip * x_rows).transpose(1, 0, 2),
        jnp.exp(a_log),
        gate_in,
    )


def solution(mesh):
    return jax.shard_map(
        local,
        mesh=mesh,
        in_specs=(
            P("inst"),
            P("inst"),
            P("inst", None, "tp"),
            P("inst", None, "tp"),
            P("inst", None, "tp"),
            P("inst", None, "tp"),
            P(None, "tp"),
            P("tp", None),
            P(None, "tp"),
            P("tp"),
            P(None, "tp"),
            P("tp"),
            P(),
        ),
        out_specs=(P("inst", None, "tp"), P("inst", None, "tp")),
        check_vma=False,
    )
```

```python
import jax
import jax.numpy as jnp
from jax import lax
from jax.experimental import pallas as pl
from jax.experimental.pallas import tpu as pltpu
from jax.sharding import PartitionSpec as P

DTR = 512
GROUPS = 12
VMEM = pl.BlockSpec(memory_space=pltpu.VMEM)
SMEM = pl.BlockSpec(memory_space=pltpu.SMEM)

ANY = pl.BlockSpec(memory_space=pl.ANY)

TILES = 3
CONV = 4


def begin(pairs, sems):
    copies = [pltpu.make_async_copy(src, dst, sems.at[i]) for i, (src, dst) in enumerate(pairs)]
    for copy in copies:
        copy.start()
    return copies


def pack_kernel(
    me_ref, anchor_hbm, target_hbm, state_hbm, conv_hbm, taps_hbm,
    leaving_ref, offset_ref, row_ref, sums_ref,
    anchor_ref, target_ref, state_ref, conv_ref, taps_ref, slot_of, rank_of, source, sems,
):
    copies = begin(
        [
            (anchor_hbm, anchor_ref),
            (target_hbm, target_ref),
            (conv_hbm, conv_ref),
            (taps_hbm, taps_ref),
            (state_hbm, state_ref),
        ],
        sems,
    )
    slots = state_ref.shape[0]
    peers = leaving_ref.shape[0]
    me = me_ref[0]
    for d in range(peers):
        for q in range(CONV):
            leaving_ref[d, 2 * TILES + q] = jnp.zeros((4, 128), jnp.float32)
    for o in range(peers):
        slot_of[o] = -1
    for copy in copies[:2]:
        copy.wait()
    for s in range(slots):
        slot_of[(target_ref[s] // slots - me + peers) % peers] = s
    rank = jnp.int32(0)
    for k in range(16):
        offset_ref[k] = 0
    for o in range(1, peers):
        slot = slot_of[o]
        rank_of[o] = rank
        offset_ref[rank] = o
        source[rank] = slot
        rank = rank + (slot >= 0).astype(jnp.int32)
    for s in range(slots):
        offset = (me - anchor_ref[s] // slots + peers) % peers
        row_ref[s] = jnp.where(offset == 0, GROUPS + anchor_ref[s] % slots, rank_of[offset])

    for copy in copies[2:4]:
        copy.wait()
    old = [conv_ref[i] for i in range(3)]
    taps = [taps_ref[i : i + 1, :] for i in range(3)]
    sums_ref[0] = old[0] * taps[0] + old[1] * taps[1] + old[2] * taps[2]
    sums_ref[1] = old[1] * taps[0] + old[2] * taps[1]
    copies[4].wait()
    for k in range(GROUPS):
        slot = source[k]
        for t in range(16):
            tile = 16 * k + t
            rows, lanes = 8 * (t // 8), 128 * (t % 8)
            block = state_ref[slot, rows : rows + 8, lanes : lanes + 128]
            for h in range(2):
                leaving_ref[tile % peers, 2 * (tile // peers) + h] = block[4 * h : 4 * h + 4]
        receiver = (me + offset_ref[k]) % peers
        for i in range(2):
            sums = sums_ref[i, pl.ds(slot, 1), :]
            for c in range(8):
                r = 8 * i + c
                leaving_ref[receiver, 2 * TILES + r // 4, r % 4 : r % 4 + 1, :] = sums[:, 128 * c : 128 * c + 128]


def pack(me, anchor, target, ssm_state, conv_state, conv_weight, peers):
    slots, _, width = ssm_state.shape
    return pl.pallas_call(
        pack_kernel,
        out_shape=(
            jax.ShapeDtypeStruct((peers, 2 * TILES + CONV, 4, 128), jnp.float32),
            jax.ShapeDtypeStruct((16,), jnp.int32),
            jax.ShapeDtypeStruct((16,), jnp.int32),
            jax.ShapeDtypeStruct((2, slots, width), jnp.float32),
        ),
        in_specs=[SMEM] + [ANY] * 5,
        out_specs=(VMEM, SMEM, SMEM, VMEM),
        scratch_shapes=[
            pltpu.SMEM(anchor.shape, jnp.int32),
            pltpu.SMEM(target.shape, jnp.int32),
            pltpu.VMEM(ssm_state.shape, jnp.float32),
            pltpu.VMEM(conv_state.shape, jnp.float32),
            pltpu.VMEM(conv_weight.shape, jnp.float32),
            pltpu.SMEM((peers,), jnp.int32),
            pltpu.SMEM((peers,), jnp.int32),
            pltpu.SMEM((16,), jnp.int32),
            pltpu.SemaphoreType.DMA((5,)),
        ],
        compiler_params=pltpu.CompilerParams(vmem_limit_bytes=56 << 20),
        name="pack",
    )(me, anchor, target, ssm_state, conv_state, conv_weight)


def roll_kernel(me_ref, offset_ref, held_ref, due_ref):
    peers = held_ref.shape[0]
    shifts = [offset_ref[4 * u + me_ref[0] // 16] for u in range(TILES)]

    def body(d, carry):
        for u, shift in enumerate(shifts):
            sender = (d - shift + peers) % peers
            for h in range(2):
                due_ref[d, 2 * u + h] = held_ref[sender, 2 * u + h]
        return carry

    lax.fori_loop(0, peers, body, 0, unroll=8)


def roll(me, offset, held):
    peers = held.shape[0]
    return pl.pallas_call(
        roll_kernel,
        out_shape=jax.ShapeDtypeStruct((peers, 2 * TILES, 4, 128), jnp.float32),
        in_specs=[SMEM, SMEM, VMEM],
        out_specs=VMEM,
        compiler_params=pltpu.CompilerParams(vmem_limit_bytes=32 << 20),
        name="roll",
    )(me, offset, held)


def update_kernel(
    row_hbm, rest_ref, moved_ref, state_ref, step_ref, x_ref, skip_ref, decay_ref, gate_ref,
    mixed_hbm, out_hbm,
    row_ref, out_ref, y_ref, gated_ref, mixed_ref, row_sem, out_sems,
):
    arriving = begin([(row_hbm, row_ref)], row_sem)
    slots, state_size, width = state_ref.shape
    steps = step_ref.shape[0]
    for s in range(slots):
        gated_ref[s] = jax.nn.silu(gate_ref[s].astype(jnp.float32))
    for copy in arriving:
        copy.wait()
    copies = []
    for s in range(slots):
        r = row_ref[s]
        b = [rest_ref[i, :state_size, s : s + 1] for i in range(steps)]
        c = [rest_ref[i, state_size:, s : s + 1] for i in range(steps)]
        rank = jnp.clip(r, 0, GROUPS - 1)
        base, group = rank % 4 * 16, rank // 4 * 2
        slot = jnp.clip(r - GROUPS, 0, slots - 1)
        for t in range(width // 128):
            cut = slice(128 * t, 128 * t + 128)
            came = [moved_ref[base + 8 * n + t, group + h] for n in range(2) for h in range(2)]
            state = jnp.where(r < GROUPS, jnp.concatenate(came), state_ref[slot, :, cut])
            decay = decay_ref[:, cut]
            for i in range(steps):
                step = step_ref[i, s : s + 1, cut]
                state = jnp.exp(-step * decay) * state + (step * x_ref[i, s : s + 1, cut]) * b[i]
                y_ref[s, i : i + 1, cut] = jnp.sum(c[i] * state, axis=0, keepdims=True)
            out_ref[s, :, cut] = state
        copies.append(pltpu.make_async_copy(out_ref.at[s], out_hbm.at[s], out_sems.at[s]))
        copies[-1].start()
        mixed_ref[s] = ((y_ref[s] + skip_ref[s]) * gated_ref[s]).astype(mixed_ref.dtype)
    copies.append(pltpu.make_async_copy(mixed_ref, mixed_hbm, out_sems.at[slots]))
    copies[-1].start()
    for copy in copies:
        copy.wait()


def update(row, rest, moved, state, step, x, skip, decay, gate):
    return pl.pallas_call(
        update_kernel,
        out_shape=(
            jax.ShapeDtypeStruct(gate.shape, jnp.bfloat16),
            jax.ShapeDtypeStruct(state.shape, jnp.float32),
        ),
        in_specs=[ANY] + [VMEM] * 8,
        out_specs=(ANY, ANY),
        scratch_shapes=[
            pltpu.SMEM(row.shape, jnp.int32),
            pltpu.VMEM(state.shape, jnp.float32),
            pltpu.VMEM(gate.shape, jnp.float32),
            pltpu.VMEM(gate.shape, jnp.float32),
            pltpu.VMEM(gate.shape, jnp.bfloat16),
            pltpu.SemaphoreType.DMA((1,)),
            pltpu.SemaphoreType.DMA((state.shape[0] + 1,)),
        ],
        compiler_params=pltpu.CompilerParams(vmem_limit_bytes=32 << 20),
        name="update",
    )(row, rest, moved, state, step, x, skip, decay, gate)


def exchange(chunks):
    return lax.all_to_all(chunks, "inst", 0, 0)


def sum_over_tp(part):
    size = lax.axis_size("tp")
    bit = 1
    while bit < size:
        part = part + lax.ppermute(part, "tp", [(i, i ^ bit) for i in range(size)])
        bit *= 2
    return part


def local(
    anchor,
    target,
    ssm_state,
    conv_state,
    x_in,
    gate_in,
    conv_weight,
    x_weight,
    dt_weight,
    dt_bias,
    a_log,
    d_skip,
    dt_gain,
):
    slots, state_size, width = ssm_state.shape
    steps = x_in.shape[1]
    taps = conv_weight.shape[0]
    peers = lax.axis_size("inst")
    me = lax.axis_index("inst").astype(jnp.int32).reshape(1)

    leaving, offset, row, sums = pack(me, anchor, target, ssm_state, conv_state.transpose(1, 0, 2), conv_weight, peers)
    spread = exchange(leaving)
    moved = exchange(roll(me, offset, spread))

    came = spread[:, 2 * TILES :].reshape(peers, steps, width)
    partial = jnp.where(
        (anchor // slots == me)[:, None, None],
        jnp.take(sums.transpose(1, 0, 2), anchor % slots, axis=0),
        jnp.take(came, anchor // slots, axis=0),
    )
    x_values = x_in.astype(jnp.float32)
    conved = []
    for i in range(steps):
        window = partial[:, i] + jnp.sum(x_values[:, : i + 1] * conv_weight[None, taps - 1 - i :], axis=1)
        conved.append(jax.nn.silu(window).astype(jnp.bfloat16))
    conved = jnp.concatenate(conved, axis=0)
    totals = sum_over_tp(jnp.dot(conved, x_weight, preferred_element_type=jnp.float32))
    dt_part = totals[:, :DTR]
    inv_rms = lax.rsqrt(jnp.mean(dt_part * dt_part, axis=-1, keepdims=True) + 1e-06)
    dt_low = (dt_part * inv_rms * dt_gain).astype(jnp.bfloat16)
    step_size = jax.nn.softplus(jnp.dot(dt_low, dt_weight, preferred_element_type=jnp.float32) + dt_bias)
    rest = totals[:, DTR:].reshape(steps, slots, 2 * state_size).transpose(0, 2, 1)
    x_rows = conved.astype(jnp.float32).reshape(steps, slots, width)
    return update(
        row,
        rest,
        moved,
        ssm_state,
        step_size.reshape(steps, slots, width),
        x_rows,
        (d_skip * x_rows).transpose(1, 0, 2),
        jnp.exp(a_log),
        gate_in,
    )


def solution(mesh):
    return jax.shard_map(
        local,
        mesh=mesh,
        in_specs=(
            P("inst"),
            P("inst"),
            P("inst", None, "tp"),
            P("inst", None, "tp"),
            P("inst", None, "tp"),
            P("inst", None, "tp"),
            P(None, "tp"),
            P("tp", None),
            P(None, "tp"),
            P("tp"),
            P(None, "tp"),
            P("tp"),
            P(),
        ),
        out_specs=(P("inst", None, "tp"), P("inst", None, "tp")),
        check_vma=False,
    )
```

```python
import jax
import jax.numpy as jnp
from jax import lax
from jax.experimental import pallas as pl
from jax.experimental.pallas import tpu as pltpu
from jax.sharding import PartitionSpec as P

DTR = 512
GROUPS = 12
VMEM = pl.BlockSpec(memory_space=pltpu.VMEM)
SMEM = pl.BlockSpec(memory_space=pltpu.SMEM)

ANY = pl.BlockSpec(memory_space=pl.ANY)

TILES = 3
CONV = 4


def begin(pairs, sems):
    copies = [pltpu.make_async_copy(src, dst, sems.at[i]) for i, (src, dst) in enumerate(pairs)]
    for copy in copies:
        copy.start()
    return copies


def pack_kernel(
    me_ref, anchor_hbm, target_hbm, state_hbm, conv_hbm, taps_hbm,
    leaving_hbm, offset_hbm, row_hbm, sums_hbm,
    leaving_ref, offset_ref, row_ref, sums_ref, anchor_ref, target_ref, state_ref, conv_ref, taps_ref, slot_of, rank_of, source, sems, out_sems,
):
    copies = begin(
        [
            (anchor_hbm, anchor_ref),
            (target_hbm, target_ref),
            (conv_hbm, conv_ref),
            (taps_hbm, taps_ref),
            (state_hbm, state_ref),
        ],
        sems,
    )
    slots = state_ref.shape[0]
    peers = leaving_ref.shape[0]
    me = me_ref[0]
    for d in range(peers):
        for q in range(CONV):
            leaving_ref[d, 2 * TILES + q] = jnp.zeros((4, 128), jnp.float32)
    for o in range(peers):
        slot_of[o] = -1
    for copy in copies[:2]:
        copy.wait()
    for s in range(slots):
        slot_of[(target_ref[s] // slots - me + peers) % peers] = s
    rank = jnp.int32(0)
    for k in range(16):
        offset_ref[k] = 0
    for o in range(1, peers):
        slot = slot_of[o]
        rank_of[o] = rank
        offset_ref[rank] = o
        source[rank] = slot
        rank = rank + (slot >= 0).astype(jnp.int32)
    for s in range(slots):
        offset = (me - anchor_ref[s] // slots + peers) % peers
        row_ref[s] = jnp.where(offset == 0, GROUPS + anchor_ref[s] % slots, rank_of[offset])

    for copy in copies[2:4]:
        copy.wait()
    old = [conv_ref[i] for i in range(3)]
    taps = [taps_ref[i : i + 1, :] for i in range(3)]
    sums_ref[0] = old[0] * taps[0] + old[1] * taps[1] + old[2] * taps[2]
    sums_ref[1] = old[1] * taps[0] + old[2] * taps[1]
    leaving = [
        pltpu.make_async_copy(offset_ref, offset_hbm, out_sems.at[0]),
        pltpu.make_async_copy(row_ref, row_hbm, out_sems.at[1]),
        pltpu.make_async_copy(sums_ref, sums_hbm, out_sems.at[2]),
    ]
    for copy in leaving:
        copy.start()

    def send(low, high):
        part = slice(low, high)
        leaving.append(
            pltpu.make_async_copy(leaving_ref.at[:, part], leaving_hbm.at[:, part], out_sems.at[len(leaving)])
        )
        leaving[-1].start()

    for k in range(GROUPS):
        receiver = (me + offset_ref[k]) % peers
        for i in range(2):
            sums = sums_ref[i, pl.ds(source[k], 1), :]
            for c in range(8):
                r = 8 * i + c
                leaving_ref[receiver, 2 * TILES + r // 4, r % 4 : r % 4 + 1, :] = sums[:, 128 * c : 128 * c + 128]
    send(2 * TILES, 2 * TILES + CONV)
    copies[4].wait()
    for u in range(TILES):
        for k in range(4 * u, 4 * u + 4):
            slot = source[k]
            for t in range(16):
                rows, lanes = 8 * (t // 8), 128 * (t % 8)
                block = state_ref[slot, rows : rows + 8, lanes : lanes + 128]
                for h in range(2):
                    leaving_ref[(16 * k + t) % peers, 2 * u + h] = block[4 * h : 4 * h + 4]
        send(2 * u, 2 * u + 2)
    for copy in leaving:
        copy.wait()


def pack(me, anchor, target, ssm_state, conv_state, conv_weight, peers):
    slots, _, width = ssm_state.shape
    return pl.pallas_call(
        pack_kernel,
        out_shape=(
            jax.ShapeDtypeStruct((peers, 2 * TILES + CONV, 4, 128), jnp.float32),
            jax.ShapeDtypeStruct((16,), jnp.int32),
            jax.ShapeDtypeStruct((16,), jnp.int32),
            jax.ShapeDtypeStruct((2, slots, width), jnp.float32),
        ),
        in_specs=[SMEM] + [ANY] * 5,
        out_specs=(ANY,) * 4,
        scratch_shapes=[
            pltpu.VMEM((peers, 2 * TILES + CONV, 4, 128), jnp.float32),
            pltpu.SMEM((16,), jnp.int32),
            pltpu.SMEM((16,), jnp.int32),
            pltpu.VMEM((2, slots, width), jnp.float32),
            pltpu.SMEM(anchor.shape, jnp.int32),
            pltpu.SMEM(target.shape, jnp.int32),
            pltpu.VMEM(ssm_state.shape, jnp.float32),
            pltpu.VMEM(conv_state.shape, jnp.float32),
            pltpu.VMEM(conv_weight.shape, jnp.float32),
            pltpu.SMEM((peers,), jnp.int32),
            pltpu.SMEM((peers,), jnp.int32),
            pltpu.SMEM((16,), jnp.int32),
            pltpu.SemaphoreType.DMA((5,)),
            pltpu.SemaphoreType.DMA((TILES + 4,)),
        ],
        compiler_params=pltpu.CompilerParams(vmem_limit_bytes=56 << 20),
        name="pack",
    )(me, anchor, target, ssm_state, conv_state, conv_weight)


def roll_kernel(me_ref, offset_ref, held_ref, due_ref):
    peers = held_ref.shape[0]
    shifts = [offset_ref[4 * u + me_ref[0] // 16] for u in range(TILES)]

    def body(d, carry):
        for u, shift in enumerate(shifts):
            sender = (d - shift + peers) % peers
            for h in range(2):
                due_ref[d, 2 * u + h] = held_ref[sender, 2 * u + h]
        return carry

    lax.fori_loop(0, peers, body, 0, unroll=8)


def roll(me, offset, held):
    peers = held.shape[0]
    return pl.pallas_call(
        roll_kernel,
        out_shape=jax.ShapeDtypeStruct((peers, 2 * TILES, 4, 128), jnp.float32),
        in_specs=[SMEM, SMEM, VMEM],
        out_specs=VMEM,
        compiler_params=pltpu.CompilerParams(vmem_limit_bytes=32 << 20),
        name="roll",
    )(me, offset, held)


def update_kernel(
    row_hbm, rest_ref, moved_ref, state_ref, step_ref, x_ref, skip_ref, decay_ref, gate_ref,
    mixed_hbm, out_hbm,
    row_ref, out_ref, y_ref, gated_ref, mixed_ref, row_sem, out_sems,
):
    arriving = begin([(row_hbm, row_ref)], row_sem)
    slots, state_size, width = state_ref.shape
    steps = step_ref.shape[0]
    for s in range(slots):
        gated_ref[s] = jax.nn.silu(gate_ref[s].astype(jnp.float32))
    for copy in arriving:
        copy.wait()
    copies = []
    for s in range(slots):
        r = row_ref[s]
        b = [rest_ref[i, :state_size, s : s + 1] for i in range(steps)]
        c = [rest_ref[i, state_size:, s : s + 1] for i in range(steps)]
        rank = jnp.clip(r, 0, GROUPS - 1)
        base, group = rank % 4 * 16, rank // 4 * 2
        slot = jnp.clip(r - GROUPS, 0, slots - 1)
        for t in range(width // 128):
            cut = slice(128 * t, 128 * t + 128)
            came = [moved_ref[base + 8 * n + t, group + h] for n in range(2) for h in range(2)]
            state = jnp.where(r < GROUPS, jnp.concatenate(came), state_ref[slot, :, cut])
            decay = decay_ref[:, cut]
            for i in range(steps):
                step = step_ref[i, s : s + 1, cut]
                state = jnp.exp(-step * decay) * state + (step * x_ref[i, s : s + 1, cut]) * b[i]
                y_ref[s, i : i + 1, cut] = jnp.sum(c[i] * state, axis=0, keepdims=True)
            out_ref[s, :, cut] = state
        copies.append(pltpu.make_async_copy(out_ref.at[s], out_hbm.at[s], out_sems.at[s]))
        copies[-1].start()
        mixed_ref[s] = ((y_ref[s] + skip_ref[s]) * gated_ref[s]).astype(mixed_ref.dtype)
    copies.append(pltpu.make_async_copy(mixed_ref, mixed_hbm, out_sems.at[slots]))
    copies[-1].start()
    for copy in copies:
        copy.wait()


def update(row, rest, moved, state, step, x, skip, decay, gate):
    return pl.pallas_call(
        update_kernel,
        out_shape=(
            jax.ShapeDtypeStruct(gate.shape, jnp.bfloat16),
            jax.ShapeDtypeStruct(state.shape, jnp.float32),
        ),
        in_specs=[ANY] + [VMEM] * 8,
        out_specs=(ANY, ANY),
        scratch_shapes=[
            pltpu.SMEM(row.shape, jnp.int32),
            pltpu.VMEM(state.shape, jnp.float32),
            pltpu.VMEM(gate.shape, jnp.float32),
            pltpu.VMEM(gate.shape, jnp.float32),
            pltpu.VMEM(gate.shape, jnp.bfloat16),
            pltpu.SemaphoreType.DMA((1,)),
            pltpu.SemaphoreType.DMA((state.shape[0] + 1,)),
        ],
        compiler_params=pltpu.CompilerParams(vmem_limit_bytes=32 << 20),
        name="update",
    )(row, rest, moved, state, step, x, skip, decay, gate)


def exchange(chunks):
    return lax.all_to_all(chunks, "inst", 0, 0)


def sum_over_tp(part):
    size = lax.axis_size("tp")
    bit = 1
    while bit < size:
        part = part + lax.ppermute(part, "tp", [(i, i ^ bit) for i in range(size)])
        bit *= 2
    return part


def local(
    anchor,
    target,
    ssm_state,
    conv_state,
    x_in,
    gate_in,
    conv_weight,
    x_weight,
    dt_weight,
    dt_bias,
    a_log,
    d_skip,
    dt_gain,
):
    slots, state_size, width = ssm_state.shape
    steps = x_in.shape[1]
    taps = conv_weight.shape[0]
    peers = lax.axis_size("inst")
    me = lax.axis_index("inst").astype(jnp.int32).reshape(1)

    leaving, offset, row, sums = pack(me, anchor, target, ssm_state, conv_state.transpose(1, 0, 2), conv_weight, peers)
    spread = exchange(leaving)
    moved = exchange(roll(me, offset, spread))

    came = spread[:, 2 * TILES :].reshape(peers, steps, width)
    partial = jnp.where(
        (anchor // slots == me)[:, None, None],
        jnp.take(sums.transpose(1, 0, 2), anchor % slots, axis=0),
        jnp.take(came, anchor // slots, axis=0),
    )
    x_values = x_in.astype(jnp.float32)
    conved = []
    for i in range(steps):
        window = partial[:, i] + jnp.sum(x_values[:, : i + 1] * conv_weight[None, taps - 1 - i :], axis=1)
        conved.append(jax.nn.silu(window).astype(jnp.bfloat16))
    conved = jnp.concatenate(conved, axis=0)
    totals = sum_over_tp(jnp.dot(conved, x_weight, preferred_element_type=jnp.float32))
    dt_part = totals[:, :DTR]
    inv_rms = lax.rsqrt(jnp.mean(dt_part * dt_part, axis=-1, keepdims=True) + 1e-06)
    dt_low = (dt_part * inv_rms * dt_gain).astype(jnp.bfloat16)
    step_size = jax.nn.softplus(jnp.dot(dt_low, dt_weight, preferred_element_type=jnp.float32) + dt_bias)
    rest = totals[:, DTR:].reshape(steps, slots, 2 * state_size).transpose(0, 2, 1)
    x_rows = conved.astype(jnp.float32).reshape(steps, slots, width)
    return update(
        row,
        rest,
        moved,
        ssm_state,
        step_size.reshape(steps, slots, width),
        x_rows,
        (d_skip * x_rows).transpose(1, 0, 2),
        jnp.exp(a_log),
        gate_in,
    )


def solution(mesh):
    return jax.shard_map(
        local,
        mesh=mesh,
        in_specs=(
            P("inst"),
            P("inst"),
            P("inst", None, "tp"),
            P("inst", None, "tp"),
            P("inst", None, "tp"),
            P("inst", None, "tp"),
            P(None, "tp"),
            P("tp", None),
            P(None, "tp"),
            P("tp"),
            P(None, "tp"),
            P("tp"),
            P(),
        ),
        out_specs=(P("inst", None, "tp"), P("inst", None, "tp")),
        check_vma=False,
    )
```
